512 devices in a mesh: section: 32 (over z_lo, y), tensor: 16 (over x, z_hi, core).
Axes of the slice: x: 4, y: 8, z: 8 (z_hi: 2, z_lo: 4; z = z_hi * 4 + z_lo), core: 2. Of those that a mesh axis runs over, the one named last changes fastest.
Arguments:
- vision_tokens: bfloat16 [2048, 1664], P('section'), may hold values from -6 to 6
- key_weight: bfloat16 [13312, 8192], P('section', 'tensor'), may hold values from -0.15625 to 0.15625
- value_weight: bfloat16 [13312, 8192], P('section', 'tensor'), may hold values from -0.15625 to 0.15625
- queries: bfloat16 [32, 1024, 8192], P('section', None, 'tensor'), may hold values from -6 to 6
- gate: float32 [8], replicated, may hold values from 0.3 to 1.5
- visible: int32 [4, 4, 4], replicated, may hold values from -1 to 1, as said below
- out_grad: bfloat16 [32, 1024, 8192], P('section', None, 'tensor'), may hold values from -6 to 6
Outputs:
- attended: bfloat16 [32, 1024, 8192], P('section', None, 'tensor')
- vision_grad: bfloat16 [2048, 1664], P('section')
The draws below stay inside these ranges and needn't reach their ends.
Inputs may be any that keep to these rules, and one draw needn't show every extreme that they name: `visible`: each row of 4 entries is non-decreasing, and every image index 0 to 1 occurs in every row.
All inputs are finite; a program needn't handle non-finite values.
Results may differ from the reference program's by a relative error of at most 0.029.
Values may be sent and summed in bfloat16 or wider, within the bound.
A program may use at most 64 MiB of HBM per device.

```python
import jax
import jax.numpy as jnp
from jax import lax

D = 8192
H = 64
HD = 128
DV = 1664
IMG_TOK = 64
TBLOCK = 64
SEQ = 256
IMGS = 2
SAMPLES = 4
MICRO = 4
TXT = 1024
VTOK = 512
LAYERS = 8


def draw_visible(key, part):
    blocks = SEQ // TBLOCK
    needed = jnp.broadcast_to(jnp.arange(IMGS, dtype=jnp.int32)[None, None, :], (MICRO, SAMPLES, IMGS))
    extra = jax.random.randint(key, (MICRO, SAMPLES, blocks - IMGS), -1, IMGS, dtype=jnp.int32)
    return jnp.sort(jnp.concatenate([needed, extra], axis=2), axis=2).astype(jnp.int32)


def block_scale(rng, extent, cuts, low, largest):
    gain, own = 1.0, jax.random.fold_in(rng, 6)
    for dim, blocks in cuts:
        heights = jnp.exp(jax.random.uniform(jax.random.fold_in(own, dim), (blocks,), jnp.float32, low / len(cuts), largest / len(cuts)))
        gain = gain * jnp.repeat(heights, extent[dim] // blocks).reshape([-1 if axis == dim else 1 for axis in range(len(extent))])
    return gain


def normal_values(key, shape, scale, limit, cuts=(), held_as=jnp.bfloat16):
    entries = scale * jax.random.normal(key, shape, jnp.float32)
    if cuts:
        entries = entries * block_scale(key, shape, cuts, -0.22, 0.18)
    return jnp.clip(entries, -limit, limit).astype(held_as)


def setup_inputs(seed: int = 0) -> dict:
    key_list = jax.random.split(jax.random.key(seed), 8)
    vision_tokens = normal_values(key_list[0], (MICRO * VTOK, DV), 1.0, 6.0, ((0, 32),))
    key_weight = normal_values(key_list[1], (MICRO * LAYERS * (DV // MICRO), D), DV ** -0.5, 0.15625, ((0, 32), (1, 16)))
    value_weight = normal_values(key_list[2], (MICRO * LAYERS * (DV // MICRO), D), DV ** -0.5, 0.15625, ((0, 32), (1, 16)))
    queries = normal_values(key_list[3], (MICRO * LAYERS, TXT, D), 1.0, 6.0, ((0, 32), (2, 16)))
    gate = jnp.clip(jax.random.uniform(key_list[4], (LAYERS,), jnp.float32, 0.3, 1.5), 0.3, 1.5)
    visible = draw_visible(jax.random.fold_in(key_list[7], 71), 0)
    out_grad = normal_values(key_list[6], (MICRO * LAYERS, TXT, D), 1.0, 6.0, ((0, 32), (2, 16)))
    return dict(vision_tokens=vision_tokens, key_weight=key_weight, value_weight=value_weight, queries=queries, gate=gate, visible=visible, out_grad=out_grad)


def block_index(visible):
    samples = visible.shape[0]
    base = jnp.arange(samples, dtype=jnp.int32)[:, None] * IMGS
    seen = (base + jnp.maximum(visible, 0)).reshape(-1).astype(jnp.int32)
    validf = (visible >= 0).reshape(-1).astype(jnp.float32)
    return seen, validf


def local_layer(key_rows, value_rows, query, gate_value, cotangent, visible, heads):
    width = heads * HD
    seen, validf = block_index(visible)
    images = key_rows.shape[0] // IMG_TOK
    key_img = key_rows.reshape(images, IMG_TOK, heads, HD)[seen]
    val_img = value_rows.reshape(images, IMG_TOK, heads, HD)[seen]
    blocks = seen.shape[0]
    query_b = query.reshape(blocks, TBLOCK, heads, HD)
    scale = 1.0 / (HD ** 0.5)
    scores = jnp.einsum("bqhd,bkhd->bhqk", query_b.astype(jnp.float32), key_img.astype(jnp.float32)) * scale
    exponent = jnp.exp(scores)
    probs = exponent / jnp.sum(exponent, axis=-1, keepdims=True) * validf[:, None, None, None]
    probs_b = probs.astype(jnp.bfloat16)
    mixed = jnp.einsum("bhqk,bkhd->bqhd", probs_b.astype(jnp.float32), val_img.astype(jnp.float32))
    factor = jnp.tanh(gate_value)
    attended = (factor * mixed).astype(jnp.bfloat16).reshape(-1, width)
    head_grad = (factor * cotangent.astype(jnp.float32)).astype(jnp.bfloat16).reshape(blocks, TBLOCK, heads, HD)
    vgrad_blk = jnp.einsum("bhqk,bqhd->bkhd", probs_b.astype(jnp.float32), head_grad.astype(jnp.float32))
    prob_grad = jnp.einsum("bqhd,bkhd->bhqk", head_grad.astype(jnp.float32), val_img.astype(jnp.float32))
    delta = jnp.sum(probs * prob_grad, axis=-1, keepdims=True)
    score_grad = (probs * (prob_grad - delta) * scale).astype(jnp.bfloat16)
    kgrad_blk = jnp.einsum("bhqk,bqhd->bkhd", score_grad.astype(jnp.float32), query_b.astype(jnp.float32))
    onehot = (seen[:, None] == jnp.arange(images, dtype=jnp.int32)[None, :]).astype(jnp.float32)
    key_grad = jnp.einsum("bi,bkhd->ikhd", onehot, kgrad_blk).reshape(-1, width).astype(jnp.bfloat16)
    value_grad = jnp.einsum("bi,bkhd->ikhd", onehot, vgrad_blk).reshape(-1, width).astype(jnp.bfloat16)
    return attended, key_grad, value_grad


def reference(vision_tokens, key_weight, value_weight, queries, gate, visible, out_grad):
    w_keys = key_weight.reshape(MICRO, LAYERS, DV // MICRO, D).transpose(1, 0, 2, 3).reshape(LAYERS, DV, D)
    w_values = value_weight.reshape(MICRO, LAYERS, DV // MICRO, D).transpose(1, 0, 2, 3).reshape(LAYERS, DV, D)
    tokens_all = vision_tokens.reshape(MICRO, VTOK, DV)
    query_all = queries.reshape(MICRO, LAYERS, TXT, D)
    grad_all = out_grad.reshape(MICRO, LAYERS, TXT, D)
    outputs = []
    grads = []
    for micro in range(MICRO):
        tokens = tokens_all[micro]
        micro_visible = visible[micro]

        def one_layer(carry, items):
            w_key, w_value, query, gate_value, cotangent = items
            key_rows = jnp.dot(tokens, w_key, preferred_element_type=jnp.float32).astype(jnp.bfloat16)
            value_rows = jnp.dot(tokens, w_value, preferred_element_type=jnp.float32).astype(jnp.bfloat16)
            attended, key_grad, value_grad = local_layer(key_rows, value_rows, query, gate_value, cotangent, micro_visible, H)
            term = lax.dot_general(key_grad, w_key, (((1,), (1,)), ((), ())), preferred_element_type=jnp.float32)
            term = term + lax.dot_general(value_grad, w_value, (((1,), (1,)), ((), ())), preferred_element_type=jnp.float32)
            return carry + term, attended

        start = jnp.zeros(tokens.shape, jnp.float32)
        total, attended = lax.scan(one_layer, start, (w_keys, w_values, query_all[micro], gate, grad_all[micro]))
        outputs.append(attended)
        grads.append(total.astype(jnp.bfloat16))
    attended_all = jnp.concatenate(outputs, axis=0)
    return attended_all, jnp.concatenate(grads, axis=0)
```

```python
import jax
import jax.numpy as jnp
from jax import lax
from jax.experimental import pallas as pl
from jax.experimental.pallas import tpu as pltpu
from jax.sharding import PartitionSpec as P

HD = 128
NZ, NY, NX = 4, 8, 4
HEADS = 4
SAMPLES = 4
QB = 416
DV = 1664
VT = 512
SHARE = 896
STEP = 768
CH = 4
PER = NY // CH
SCALE = 1.0 / HD**0.5
MESH = pl.DeviceIdType.MESH
F32 = jnp.float32
BF16 = jnp.bfloat16


def nt(a, b):
    return lax.dot_general(a, b, (((1,), (1,)), ((), ())), preferred_element_type=F32)


def nn(a, b):
    return lax.dot_general(a, b, (((1,), (0,)), ((), ())), preferred_element_type=F32)


def tn(a, b):
    return lax.dot_general(a, b, (((0,), (0,)), ((), ())), preferred_element_type=F32)


def kernel(
    gate, visible, vision, wk, wv, query, cot, att_out, vis_out,
    wbuf, xbuf, qbuf, gbuf, abuf, bias, kvbuf, dkv, acc,
    s1, r1, xs, xr, ys, yr, zs, zr, fs, ar, obuf,
    lsem, lw, lq, lg, lo,
    zsend, zrecv, xsend, xrecv, xsib,
    s1s, s1r, b2s, b2r, b3s, b3r, b4s, b4r, b5s, b5r,
):
    section = lax.axis_index("section")
    tensor = lax.axis_index("tensor")
    p = section // NY
    y = section % NY
    x = tensor // 4
    zh = (tensor // 2) % 2
    c = tensor % 2
    sib = (section, tensor + 1 - 2 * c)

    def at_y(d):
        return (p * NY + lax.rem(y + d, NY), tensor)

    def at_x(d, core):
        return (section, lax.rem(x + d, NX) * 4 + zh * 2 + core)

    partner = (section, x * 4 + (1 - zh) * 2 + c)

    own_x = pltpu.make_async_copy(vision, xbuf.at[pl.ds(y * 64, 64)], lsem.at[0])
    own_x.start()

    def local_w(h, kv):
        ref = wv if kv else wk
        return pltpu.make_async_copy(
            ref.at[:, pl.ds(h * HD, HD)],
            wbuf.at[h, pl.ds(p * QB, QB), pl.ds(kv * HD, HD)],
            lw.at[h, kv],
        )

    for h in range(HEADS):
        local_w(h, 0).start()
        local_w(h, 1).start()

    def local_q(h):
        return pltpu.make_async_copy(query.at[0, :, pl.ds(h * HD, HD)], qbuf.at[h], lq.at[h])

    def local_g(h):
        return pltpu.make_async_copy(cot.at[0, :, pl.ds(h * HD, HD)], gbuf.at[h], lg.at[h])

    for h in range(HEADS):
        local_q(h).start()
        local_g(h).start()

    barrier = pltpu.get_barrier_semaphore()

    def greet(device):
        pl.semaphore_signal(barrier, inc=1, device_id=device, device_id_type=MESH)

    has_left = p > 0
    has_right = p < NZ - 1

    @pl.when(has_left)
    def _():
        greet((section - NY, tensor))

    @pl.when(has_right)
    def _():
        greet((section + NY, tensor))

    for d in range(1, NY):
        greet(at_y(d))
    for d in range(1, NX):
        greet(at_x(d, c))
    for d in range(NX):
        greet(at_x(d, 1 - c))
    greet(partner)
    ends = jnp.where(has_left, 1, 0) + jnp.where(has_right, 1, 0)
    pl.semaphore_wait(barrier, 15 + ends)

    def zcopy(q, h, right):
        rows = pl.ds(pl.multiple_of(q * QB, 16), QB)
        return pltpu.make_async_remote_copy(
            src_ref=wbuf.at[h, rows],
            dst_ref=wbuf.at[h, rows],
            send_sem=zsend.at[right, q, h],
            recv_sem=zrecv.at[q, h],
            device_id=(section + (NY if right else -NY), tensor),
            device_id_type=MESH,
        )

    for h in range(HEADS):
        local_w(h, 0).wait()
        local_w(h, 1).wait()

        @pl.when(has_left)
        def _():
            zcopy(p, h, 0).start()

        @pl.when(has_right)
        def _():
            zcopy(p, h, 1).start()

    def xcopy(source, to, core):
        rows = pl.ds(pl.multiple_of(source * 64 + core * 32, 32), 32)
        return pltpu.make_async_remote_copy(
            src_ref=xbuf.at[rows],
            dst_ref=xbuf.at[rows],
            send_sem=xsend.at[to, source],
            recv_sem=xsib.at[source] if to == 2 else xrecv.at[source],
            device_id=(at_y(1), at_y(NY - 1), sib)[to],
            device_id_type=MESH,
        )

    own_x.wait()
    xcopy(y, 0, c).start()
    xcopy(y, 1, c).start()

    lane = lax.broadcasted_iota(jnp.int32, (128, 256), 1)
    image = lax.broadcasted_iota(jnp.int32, (128, 256), 0) // 64
    for s in range(SAMPLES):
        seen = jnp.where(
            lane < 128,
            jnp.where(lane < 64, visible[p, s, 0], visible[p, s, 1]),
            jnp.where(lane < 192, visible[p, s, 2], visible[p, s, 3]),
        )
        bias[s] = jnp.where(seen == image, 0.0, -1e30).astype(F32)
    acc[...] = jnp.zeros_like(acc)

    for t in range(1, 5):
        below = lax.rem(y + NY - t, NY)
        xcopy(below, 0, c).wait_recv()
        if t < 4:
            xcopy(below, 0, c).start()
        xcopy(below, 2, c).start()
        if t < 4:
            above = lax.rem(y + t, NY)
            xcopy(above, 1, c).wait_recv()
            if t < 3:
                xcopy(above, 1, c).start()
            xcopy(above, 2, c).start()
    for t in range(1, NY):
        source = lax.rem(y + t, NY)
        xcopy(source, 2, 1 - c).wait_recv()
    factor = jnp.tanh(jnp.full((1, HD), gate[y], F32))

    def one_head(h, carry):
        for d in range(1, NZ):

            @pl.when(p + d < NZ)
            def _():
                q = p + d
                zcopy(q, h, 0).wait_recv()

                @pl.when(has_left)
                def _():
                    zcopy(q, h, 0).start()

            @pl.when(p - d >= 0)
            def _():
                q = p - d
                zcopy(q, h, 1).wait_recv()

                @pl.when(has_right)
                def _():
                    zcopy(q, h, 1).start()

        local_q(h).wait()
        local_g(h).wait()
        kvbuf[...] = nn(xbuf[...], wbuf[h]).astype(BF16)
        for s in range(SAMPLES):
            keys = kvbuf[pl.ds(s * 128, 128), :HD]
            values = kvbuf[pl.ds(s * 128, 128), HD:]
            qs = qbuf[h, pl.ds(s * 256, 256)]
            hg = (factor * gbuf[h, pl.ds(s * 256, 256)].astype(F32)).astype(BF16)
            e = jnp.exp(nt(keys, qs) * SCALE + bias[s])
            total = jnp.sum(e, axis=0, keepdims=True)
            probs = e * (1.0 / jnp.where(total > 0.0, total, 1.0))
            probs_b = probs.astype(BF16)
            abuf[h, pl.ds(s * 256, 256)] = (factor * tn(probs_b, values)).astype(BF16)
            dkv[pl.ds(s * 128, 128), HD:] = nn(probs_b, hg).astype(BF16)
            pg = nt(values, hg)
            delta = jnp.sum(probs * pg, axis=0, keepdims=True)
            sg = (probs * (pg - delta) * SCALE).astype(BF16)
            dkv[pl.ds(s * 128, 128), :HD] = nn(sg, qs).astype(BF16)
        out_copy(h).start()
        acc[...] += nt(dkv[...], wbuf[h])
        return carry

    def out_copy(h):
        return pltpu.make_async_copy(abuf.at[h], att_out.at[0, :, pl.ds(h * HD, HD)], lo.at[h])

    lax.fori_loop(0, HEADS, one_head, 0)

    def b1(k):
        return pltpu.make_async_remote_copy(
            src_ref=s1.at[k], dst_ref=r1.at[k], send_sem=s1s.at[k], recv_sem=s1r.at[k],
            device_id=sib, device_id_type=MESH,
        )

    for k in range(CH):
        for j in range(PER):
            o = k + CH * j
            start = pl.multiple_of(o * 64 + (1 - c) * 32, 32)
            s1[k, j] = acc[pl.ds(start, 32)].astype(BF16)
        b1(k).start()

    def b2(k, d):
        peer = lax.rem(x + d, NX)
        row = pl.multiple_of((peer // 2) * 16, 16)
        col = pl.multiple_of((peer % 2) * STEP, 128)
        return pltpu.make_async_remote_copy(
            src_ref=xs.at[k, :, pl.ds(row, 16), pl.ds(col, SHARE)],
            dst_ref=xr.at[k, d - 1],
            send_sem=b2s.at[k, d - 1], recv_sem=b2r.at[k, d - 1],
            device_id=at_x(d, c), device_id_type=MESH,
        )

    for k in range(CH):
        b1(k).wait_recv()
        for j in range(PER):
            o = k + CH * j
            start = pl.multiple_of(o * 64 + c * 32, 32)
            xs[k, j] = (acc[pl.ds(start, 32)] + r1[k, j].astype(F32)).astype(BF16)
        for d in (2, 1, 3):
            b2(k, d).start()

    my_row = pl.multiple_of((x // 2) * 16, 16)
    my_col = pl.multiple_of((x % 2) * STEP, 128)

    def b3(k, j):
        return pltpu.make_async_remote_copy(
            src_ref=ys.at[k, j], dst_ref=yr.at[y],
            send_sem=b3s.at[k, j], recv_sem=b3r.at[y],
            device_id=(p * NY + k + CH * j, tensor), device_id_type=MESH,
        )

    for k in range(CH):
        for d in range(1, NX):
            b2(k, d).wait_recv()
        part = xs[k, :, pl.ds(my_row, 16), pl.ds(my_col, SHARE)].astype(F32)
        for d in range(NX - 1):
            part = part + xr[k, d].astype(F32)
        ys[k] = part.astype(BF16)
        for j in range(PER):

            @pl.when(y != k + CH * j)
            def _():
                b3(k, j).start()

    total = ys[y % CH, y // CH].astype(F32)
    for d in range(1, NY):
        source = lax.rem(y + d, NY)
        pltpu.make_async_remote_copy(
            src_ref=ys.at[0, 0], dst_ref=yr.at[source],
            send_sem=b3s.at[0, 0], recv_sem=b3r.at[source],
            device_id=at_y(d), device_id_type=MESH,
        ).wait_recv()
        total = total + yr[source].astype(F32)
    zs[...] = total.astype(BF16)
    b4 = pltpu.make_async_remote_copy(
        src_ref=zs, dst_ref=zr, send_sem=b4s, recv_sem=b4r, device_id=partner, device_id_type=MESH
    )
    b4.start()
    b4.wait_recv()
    fs[...] = (zs[...].astype(F32) + zr[...].astype(F32)).astype(BF16)

    def b5(d, other):
        core = 1 - c if other else c
        return pltpu.make_async_remote_copy(
            src_ref=fs, dst_ref=ar.at[c, x],
            send_sem=b5s.at[other, d], recv_sem=b5r.at[c, x],
            device_id=at_x(d, core), device_id_type=MESH,
        )

    everyone = [(d, o) for d in (2, 1, 3, 0) for o in (0, 1) if (d, o) != (0, 0)]
    for d, o in everyone:
        b5(d, o).start()
    ar[c, x] = fs[...]
    for d, o in everyone:
        core = 1 - c if o else c
        source = lax.rem(x + d, NX)
        pltpu.make_async_remote_copy(
            src_ref=fs, dst_ref=ar.at[core, source],
            send_sem=b5s.at[o, d], recv_sem=b5r.at[core, source],
            device_id=at_x(d, core), device_id_type=MESH,
        ).wait_recv()
    for core in range(2):
        for i in range(2):
            rows = pl.ds(core * 32 + i * 16, 16)
            obuf[rows, pl.ds(0, SHARE)] = ar[core, 2 * i]
            obuf[rows, pl.ds(SHARE, DV - SHARE)] = ar[core, 2 * i + 1, :, pl.ds(SHARE - STEP, DV - SHARE)]
    last = pltpu.make_async_copy(obuf, vis_out, lsem.at[1])
    last.start()

    for h in range(HEADS):
        for q in range(NZ):

            @pl.when(jnp.logical_and(has_left, p <= q))
            def _():
                zcopy(q, h, 0).wait_send()

            @pl.when(jnp.logical_and(has_right, p >= q))
            def _():
                zcopy(q, h, 1).wait_send()

    xcopy(y, 0, c).wait_send()
    xcopy(y, 1, c).wait_send()
    for t in range(1, 5):
        below = lax.rem(y + NY - t, NY)
        if t < 4:
            xcopy(below, 0, c).wait_send()
        xcopy(below, 2, c).wait_send()
        if t < 4:
            above = lax.rem(y + t, NY)
            if t < 3:
                xcopy(above, 1, c).wait_send()
            xcopy(above, 2, c).wait_send()
    for k in range(CH):
        b1(k).wait_send()
        for d in range(1, NX):
            b2(k, d).wait_send()
        for j in range(PER):

            @pl.when(y != k + CH * j)
            def _():
                b3(k, j).wait_send()

    b4.wait_send()
    for d, o in everyone:
        b5(d, o).wait_send()
    for h in range(HEADS):
        out_copy(h).wait()
    last.wait()


def shards(vision_tokens, key_weight, value_weight, queries, gate, visible, out_grad):
    dma = pltpu.SemaphoreType.DMA
    hbm = pl.BlockSpec(memory_space=pl.ANY)
    smem = pl.BlockSpec(memory_space=pltpu.SMEM)
    return pl.pallas_call(
        kernel,
        out_shape=(
            jax.ShapeDtypeStruct(queries.shape, BF16),
            jax.ShapeDtypeStruct(vision_tokens.shape, BF16),
        ),
        in_specs=[smem, smem, hbm, hbm, hbm, hbm, hbm],
        out_specs=(hbm, hbm),
        scratch_shapes=[
            pltpu.VMEM((HEADS, DV, 2 * HD), BF16),
            pltpu.VMEM((VT, DV), BF16),
            pltpu.VMEM((HEADS, 1024, HD), BF16),
            pltpu.VMEM((HEADS, 1024, HD), BF16),
            pltpu.VMEM((HEADS, 1024, HD), BF16),
            pltpu.VMEM((SAMPLES, 128, 256), F32),
            pltpu.VMEM((VT, 2 * HD), BF16),
            pltpu.VMEM((VT, 2 * HD), BF16),
            pltpu.VMEM((VT, DV), F32),
            pltpu.VMEM((CH, PER, 32, DV), BF16),
            pltpu.VMEM((CH, PER, 32, DV), BF16),
            pltpu.VMEM((CH, PER, 32, DV), BF16),
            pltpu.VMEM((CH, NX - 1, PER, 16, SHARE), BF16),
            pltpu.VMEM((CH, PER, 16, SHARE), BF16),
            pltpu.VMEM((NY, 16, SHARE), BF16),
            pltpu.VMEM((16, SHARE), BF16),
            pltpu.VMEM((16, SHARE), BF16),
            pltpu.VMEM((16, SHARE), BF16),
            pltpu.VMEM((2, NX, 16, SHARE), BF16),
            pltpu.VMEM((64, DV), BF16),
            dma((2,)),
            dma((HEADS, 2)),
            dma((HEADS,)),
            dma((HEADS,)),
            dma((HEADS,)),
            dma((2, NZ, HEADS)),
            dma((NZ, HEADS)),
            dma((3, NY)),
            dma((NY,)),
            dma((NY,)),
            dma((CH,)),
            dma((CH,)),
            dma((CH, NX - 1)),
            dma((CH, NX - 1)),
            dma((CH, PER)),
            dma((NY,)),
            dma,
            dma,
            dma((2, NX)),
            dma((2, NX)),
        ],
        compiler_params=pltpu.CompilerParams(
            collective_id=0, has_side_effects=True, vmem_limit_bytes=48 * 2**20
        ),
        cost_estimate=pl.CostEstimate(flops=4 * 10**9, bytes_accessed=5 * 10**6, transcendentals=2**19),
    )(gate, visible, vision_tokens, key_weight, value_weight, queries, out_grad)


def solution(mesh):
    placed = (
        P("section", None),
        P("section", "tensor"),
        P("section", "tensor"),
        P("section", None, "tensor"),
        P(),
        P(),
        P("section", None, "tensor"),
    )
    return jax.shard_map(
        shards,
        mesh=mesh,
        in_specs=placed,
        out_specs=(P("section", None, "tensor"), P("section", None)),
        check_vma=False,
    )
```

```python
import jax
import jax.numpy as jnp
from jax import lax
from jax.experimental import pallas as pl
from jax.experimental.pallas import tpu as pltpu
from jax.sharding import PartitionSpec as P

HD = 128
NZ, NY, NX = 4, 8, 4
HEADS = 4
SAMPLES = 4
QB = 416
DV = 1664
VT = 512
SHARE = 896
STEP = 768
SCALE = 1.0 / HD**0.5
MESH = pl.DeviceIdType.MESH
F32 = jnp.float32
BF16 = jnp.bfloat16


def nt(a, b):
    return lax.dot_general(a, b, (((1,), (1,)), ((), ())), preferred_element_type=F32)


def nn(a, b):
    return lax.dot_general(a, b, (((1,), (0,)), ((), ())), preferred_element_type=F32)


def tn(a, b):
    return lax.dot_general(a, b, (((0,), (0,)), ((), ())), preferred_element_type=F32)


def reduction(acc, bufs, sems, place, peers):
    s1, r1, xs, xr, ys, yr, zs, zr, fs, ar = bufs
    sent, sent_all, got_pair, got_x, got_y, got_plane, got_all = sems
    section, p, y, x, c = place
    sib, partner, at_y, at_x = peers
    everyone = [(d, o) for d in (2, 1, 3, 0) for o in (0, 1) if (d, o) != (0, 0)]
    my_row = pl.multiple_of((x // 2) * 16, 16)
    my_col = pl.multiple_of((x % 2) * STEP, 128)

    def remote(src, dst, send, recv, device):
        return pltpu.make_async_remote_copy(
            src_ref=src, dst_ref=dst, send_sem=send, recv_sem=recv, device_id=device, device_id_type=MESH
        )

    def half(k, j, core):
        return pl.ds(pl.multiple_of((sample_at(y, k) * 2 + j) * 64 + core * 32, 32), 32)

    def b1(k):
        return remote(s1.at[k], r1.at[k], sent.at[k, 0], got_pair.at[k], sib)

    def pair(k):
        for j in range(2):
            s1[k, j] = acc[half(k, j, 1 - c)].astype(BF16)
        b1(k).start()

    def b2(k, d):
        peer = lax.rem(x + d, NX)
        row = pl.multiple_of((peer // 2) * 16, 16)
        col = pl.multiple_of((peer % 2) * STEP, 128)
        return remote(
            xs.at[k, :, pl.ds(row, 16), pl.ds(col, SHARE)], xr.at[k, d - 1],
            sent.at[k, d], got_x.at[k, d - 1], at_x(d, c),
        )

    def along_x(k):
        b1(k).wait_recv()
        for j in range(2):
            xs[k, j] = (acc[half(k, j, c)] + r1[k, j].astype(F32)).astype(BF16)
        for d in (2, 1, 3):
            b2(k, d).start()

    def b3(k, j):
        owner = (p * NY + sample_at(y, k) * 2 + j, lax.axis_index("tensor"))
        return remote(ys.at[k, j], yr.at[y], sent.at[k, 4 + j], got_y.at[y], owner)

    def owners(k):
        return (0, 1) if k < SAMPLES - 1 else (1 - y % 2,)

    def along_y(k):
        for d in range(1, NX):
            b2(k, d).wait_recv()
        total = xs[k, :, pl.ds(my_row, 16), pl.ds(my_col, SHARE)].astype(F32)
        for d in range(NX - 1):
            total = total + xr[k, d].astype(F32)
        ys[k] = total.astype(BF16)
        for j in owners(k):
            b3(k, j).start()

    def b4():
        return remote(zs, zr, sent_all.at[0], got_plane, partner)

    def planes():
        total = ys[SAMPLES - 1, y % 2].astype(F32)
        for d in (4, 3, 5, 2, 6, 1, 7):
            source = lax.rem(y + d, NY)
            remote(ys.at[0, 0], yr.at[source], sent.at[0, 4], got_y.at[source], at_y(d)).wait_recv()
            total = total + yr[source].astype(F32)
        zs[...] = total.astype(BF16)
        b4().start()

    def b5(d, other, core, source):
        return remote(
            fs, ar.at[core, source], sent_all.at[d * 2 + other], got_all.at[core, source],
            at_x(d, 1 - c if other else c),
        )

    def spread():
        b4().wait_recv()
        fs[...] = (zs[...].astype(F32) + zr[...].astype(F32)).astype(BF16)
        for d, o in everyone:
            b5(d, o, c, x).start()
        ar[c, x] = fs[...]

    def collect(out):
        for d, o in everyone:
            b5(d, o, 1 - c if o else c, lax.rem(x + d, NX)).wait_recv()
        for core in range(2):
            for i in range(2):
                rows = pl.ds(core * 32 + i * 16, 16)
                out[rows, pl.ds(0, SHARE)] = ar[core, 2 * i]
                out[rows, pl.ds(SHARE, DV - SHARE)] = ar[core, 2 * i + 1, :, pl.ds(SHARE - STEP, DV - SHARE)]

    def all_sent():
        for k in range(SAMPLES):
            b1(k).wait_send()
            for d in range(1, NX):
                b2(k, d).wait_send()
            for j in owners(k):
                b3(k, j).wait_send()
        b4().wait_send()
        for d, o in everyone:
            b5(d, o, c, x).wait_send()

    return dict(
        pair=pair, along_x=along_x, along_y=along_y, planes=planes, spread=spread, collect=collect, sent=all_sent
    )


def sample_at(y, k):
    return lax.rem(y // 2 + 1 + k, SAMPLES)


def reduction_bufs():
    shapes = [(SAMPLES, 2, 32, DV)] * 3 + [(SAMPLES, NX - 1, 2, 16, SHARE), (SAMPLES, 2, 16, SHARE)]
    shapes += [(NY, 16, SHARE)] + [(16, SHARE)] * 3 + [(2, NX, 16, SHARE)]
    return [pltpu.VMEM(shape, BF16) for shape in shapes]


def reduction_sems():
    dma = pltpu.SemaphoreType.DMA
    shapes = [(SAMPLES, 6), (8,), (SAMPLES,), (SAMPLES, NX - 1), (NY,)]
    return [dma(shape) for shape in shapes] + [dma, dma((2, NX))]


def kernel(
    gate, visible, vision, wk, wv, query, cot, att_out, vis_out,
    wbuf, xbuf, qbuf, gbuf, abuf, bias, kvbuf, dkv, acc,
    obuf, bufs, lsem, lw, lq, lg, lo, zsend, zrecv, xsend, xrecv, xsib, sems,
):
    section = lax.axis_index("section")
    tensor = lax.axis_index("tensor")
    p = section // NY
    y = section % NY
    x = tensor // 4
    zh = (tensor // 2) % 2
    c = tensor % 2
    sib = (section, tensor + 1 - 2 * c)

    def at_y(d):
        return (p * NY + lax.rem(y + d, NY), tensor)

    def at_x(d, core):
        return (section, lax.rem(x + d, NX) * 4 + zh * 2 + core)

    partner = (section, x * 4 + (1 - zh) * 2 + c)

    own_x = pltpu.make_async_copy(vision, xbuf.at[pl.ds(y * 64, 64)], lsem.at[0])
    own_x.start()

    def local_w(h, kv):
        ref = wv if kv else wk
        return pltpu.make_async_copy(
            ref.at[:, pl.ds(h * HD, HD)],
            wbuf.at[h, pl.ds(p * QB, QB), pl.ds(kv * HD, HD)],
            lw.at[h, kv],
        )

    for h in range(HEADS):
        local_w(h, 0).start()
        local_w(h, 1).start()

    def local_q(h):
        return pltpu.make_async_copy(query.at[0, :, pl.ds(h * HD, HD)], qbuf.at[h], lq.at[h])

    def local_g(h):
        return pltpu.make_async_copy(cot.at[0, :, pl.ds(h * HD, HD)], gbuf.at[h], lg.at[h])

    for h in range(HEADS):
        local_q(h).start()
        local_g(h).start()

    barrier = pltpu.get_barrier_semaphore()

    def greet(device):
        pl.semaphore_signal(barrier, inc=1, device_id=device, device_id_type=MESH)

    has_left = p > 0
    has_right = p < NZ - 1

    @pl.when(has_left)
    def _():
        greet((section - NY, tensor))

    @pl.when(has_right)
    def _():
        greet((section + NY, tensor))

    for d in range(1, NY):
        greet(at_y(d))
    for d in range(1, NX):
        greet(at_x(d, c))
    for d in range(NX):
        greet(at_x(d, 1 - c))
    greet(partner)
    ends = jnp.where(has_left, 1, 0) + jnp.where(has_right, 1, 0)
    pl.semaphore_wait(barrier, 15 + ends)

    def zcopy(q, h, right):
        rows = pl.ds(pl.multiple_of(q * QB, 16), QB)
        return pltpu.make_async_remote_copy(
            src_ref=wbuf.at[h, rows],
            dst_ref=wbuf.at[h, rows],
            send_sem=zsend.at[right, q, h],
            recv_sem=zrecv.at[q, h],
            device_id=(section + (NY if right else -NY), tensor),
            device_id_type=MESH,
        )

    for h in range(HEADS):
        local_w(h, 0).wait()
        local_w(h, 1).wait()

        @pl.when(has_left)
        def _():
            zcopy(p, h, 0).start()

        @pl.when(has_right)
        def _():
            zcopy(p, h, 1).start()

    def relay(d, h):
        @pl.when(p + d < NZ)
        def _():
            q = p + d
            zcopy(q, h, 0).wait_recv()

            @pl.when(has_left)
            def _():
                zcopy(q, h, 0).start()

        @pl.when(p - d >= 0)
        def _():
            q = p - d
            zcopy(q, h, 1).wait_recv()

            @pl.when(has_right)
            def _():
                zcopy(q, h, 1).start()

    def xcopy(source, to, core):
        rows = pl.ds(pl.multiple_of(source * 64 + core * 32, 32), 32)
        return pltpu.make_async_remote_copy(
            src_ref=xbuf.at[rows],
            dst_ref=xbuf.at[rows],
            send_sem=xsend.at[to, source],
            recv_sem=xsib.at[source] if to == 2 else xrecv.at[source],
            device_id=(at_y(1), at_y(NY - 1), sib)[to],
            device_id_type=MESH,
        )

    own_x.wait()
    xcopy(y, 0, c).start()
    xcopy(y, 1, c).start()

    lane = lax.broadcasted_iota(jnp.int32, (128, 256), 1)
    image = lax.broadcasted_iota(jnp.int32, (128, 256), 0) // 64
    for s in range(SAMPLES):
        seen = jnp.where(
            lane < 128,
            jnp.where(lane < 64, visible[p, s, 0], visible[p, s, 1]),
            jnp.where(lane < 192, visible[p, s, 2], visible[p, s, 3]),
        )
        bias[s] = jnp.where(seen == image, 0.0, -1e30).astype(F32)
    acc[...] = jnp.zeros_like(acc)

    for t in range(1, 5):
        below = lax.rem(y + NY - t, NY)
        xcopy(below, 0, c).wait_recv()
        if t < 4:
            xcopy(below, 0, c).start()
        xcopy(below, 2, c).start()
        if t < 4:
            above = lax.rem(y + t, NY)
            xcopy(above, 1, c).wait_recv()
            if t < 3:
                xcopy(above, 1, c).start()
            xcopy(above, 2, c).start()
        relay(1, t - 1)
    for t in range(1, NY):
        source = lax.rem(y + t, NY)
        xcopy(source, 2, 1 - c).wait_recv()
    factor = jnp.tanh(jnp.full((1, HD), gate[y], F32))

    def ready(h):
        for d in range(2, NZ):
            relay(d, h)
        local_q(h).wait()
        local_g(h).wait()
        kvbuf[...] = nn(xbuf[...], wbuf[h]).astype(BF16)

    def attend(h, s):
        image_rows = pl.ds(pl.multiple_of(s * 128, 128), 128)
        text_rows = pl.ds(pl.multiple_of(s * 256, 256), 256)
        keys = kvbuf[image_rows, :HD]
        values = kvbuf[image_rows, HD:]
        qs = qbuf[h, text_rows]
        hg = (factor * gbuf[h, text_rows].astype(F32)).astype(BF16)
        e = jnp.exp(nt(keys, qs) * SCALE + bias[s])
        total = jnp.sum(e, axis=0, keepdims=True)
        probs = e * (1.0 / jnp.where(total > 0.0, total, 1.0))
        probs_b = probs.astype(BF16)
        abuf[h, text_rows] = (factor * tn(probs_b, values)).astype(BF16)
        dkv[image_rows, HD:] = nn(probs_b, hg).astype(BF16)
        pg = nt(values, hg)
        delta = jnp.sum(probs * pg, axis=0, keepdims=True)
        sg = (probs * (pg - delta) * SCALE).astype(BF16)
        dkv[image_rows, :HD] = nn(sg, qs).astype(BF16)

    def one_head(h, carry):
        ready(h)
        for s in range(SAMPLES):
            attend(h, s)
        out_copy(h).start()
        acc[...] += nt(dkv[...], wbuf[h])
        return carry

    def out_copy(h):
        return pltpu.make_async_copy(abuf.at[h], att_out.at[0, :, pl.ds(h * HD, HD)], lo.at[h])

    lax.fori_loop(0, HEADS - 1, one_head, 0)

    reduce = reduction(acc, bufs, sems, (section, p, y, x, c), (sib, partner, at_y, at_x))
    ready(HEADS - 1)
    for k in range(SAMPLES):
        s = sample_at(y, k)
        attend(HEADS - 1, s)
        rows = pl.ds(pl.multiple_of(s * 128, 128), 128)
        acc[rows] += nt(dkv[rows], wbuf[HEADS - 1])
        reduce["pair"](k)
        if k:
            reduce["along_x"](k - 1)
    reduce["along_x"](SAMPLES - 1)
    out_copy(HEADS - 1).start()
    for k in range(SAMPLES):
        reduce["along_y"](k)
    reduce["planes"]()
    reduce["spread"]()
    reduce["collect"](obuf)
    last = pltpu.make_async_copy(obuf, vis_out, lsem.at[1])
    last.start()

    for h in range(HEADS):
        for q in range(NZ):

            @pl.when(jnp.logical_and(has_left, p <= q))
            def _():
                zcopy(q, h, 0).wait_send()

            @pl.when(jnp.logical_and(has_right, p >= q))
            def _():
                zcopy(q, h, 1).wait_send()

    xcopy(y, 0, c).wait_send()
    xcopy(y, 1, c).wait_send()
    for t in range(1, 5):
        below = lax.rem(y + NY - t, NY)
        if t < 4:
            xcopy(below, 0, c).wait_send()
        xcopy(below, 2, c).wait_send()
        if t < 4:
            above = lax.rem(y + t, NY)
            if t < 3:
                xcopy(above, 1, c).wait_send()
            xcopy(above, 2, c).wait_send()
    reduce["sent"]()
    for h in range(HEADS):
        out_copy(h).wait()
    last.wait()


def shards(vision_tokens, key_weight, value_weight, queries, gate, visible, out_grad):
    dma = pltpu.SemaphoreType.DMA
    hbm = pl.BlockSpec(memory_space=pltpu.HBM)
    smem = pl.BlockSpec(memory_space=pltpu.SMEM)
    return pl.pallas_call(
        kernel,
        out_shape=(
            jax.ShapeDtypeStruct(queries.shape, BF16),
            jax.ShapeDtypeStruct(vision_tokens.shape, BF16),
        ),
        in_specs=[smem, smem, hbm, hbm, hbm, hbm, hbm],
        out_specs=(pl.BlockSpec(memory_space=pl.ANY),) * 2,
        scratch_shapes=[
            pltpu.VMEM((HEADS, DV, 2 * HD), BF16),
            pltpu.VMEM((VT, DV), BF16),
            pltpu.VMEM((HEADS, 1024, HD), BF16),
            pltpu.VMEM((HEADS, 1024, HD), BF16),
            pltpu.VMEM((HEADS, 1024, HD), BF16),
            pltpu.VMEM((SAMPLES, 128, 256), F32),
            pltpu.VMEM((VT, 2 * HD), BF16),
            pltpu.VMEM((VT, 2 * HD), BF16),
            pltpu.VMEM((VT, DV), F32),
            pltpu.VMEM((64, DV), BF16),
            reduction_bufs(),
            dma((2,)),
            dma((HEADS, 2)),
            dma((HEADS,)),
            dma((HEADS,)),
            dma((HEADS,)),
            dma((2, NZ, HEADS)),
            dma((NZ, HEADS)),
            dma((3, NY)),
            dma((NY,)),
            dma((NY,)),
            reduction_sems(),
        ],
        compiler_params=pltpu.CompilerParams(
            collective_id=0, has_side_effects=True, vmem_limit_bytes=60 * 2**20
        ),
        cost_estimate=pl.CostEstimate(flops=4 * 10**9, bytes_accessed=5 * 10**6, transcendentals=2**19),
    )(gate, visible, vision_tokens, key_weight, value_weight, queries, out_grad)


def solution(mesh):
    placed = (
        P("section", None),
        P("section", "tensor"),
        P("section", "tensor"),
        P("section", None, "tensor"),
        P(),
        P(),
        P("section", None, "tensor"),
    )
    return jax.shard_map(
        shards,
        mesh=mesh,
        in_specs=placed,
        out_specs=(P("section", None, "tensor"), P("section", None)),
        check_vma=False,
    )
```

```python
import jax
import jax.numpy as jnp
from jax import lax
from jax.experimental import pallas as pl
from jax.experimental.pallas import tpu as pltpu
from jax.sharding import PartitionSpec as P

HD = 128
NZ, NY, NX = 4, 8, 4
HEADS = 4
SAMPLES = 4
QB = 416
DV = 1664
VT = 512
SHARE = 896
STEP = 768
SCALE = 1.0 / HD**0.5
MESH = pl.DeviceIdType.MESH
F32 = jnp.float32
BF16 = jnp.bfloat16


def nt(a, b):
    return lax.dot_general(a, b, (((1,), (1,)), ((), ())), preferred_element_type=F32)


def nn(a, b):
    return lax.dot_general(a, b, (((1,), (0,)), ((), ())), preferred_element_type=F32)


def tn(a, b):
    return lax.dot_general(a, b, (((0,), (0,)), ((), ())), preferred_element_type=F32)


def reduction(acc, bufs, sems, place, peers):
    s1, r1, xs, xr, ys, yr, zs, zr, fs, ar = bufs
    sent, sent_all, got_pair, got_x, got_y, got_plane, got_all = sems
    section, p, y, x, c = place
    sib, partner, at_y, at_x = peers
    everyone = [(d, o) for d in (2, 1, 3, 0) for o in (0, 1) if (d, o) != (0, 0)]
    my_row = pl.multiple_of((x // 2) * 16, 16)
    my_col = pl.multiple_of((x % 2) * STEP, 128)

    def remote(src, dst, send, recv, device):
        return pltpu.make_async_remote_copy(
            src_ref=src, dst_ref=dst, send_sem=send, recv_sem=recv, device_id=device, device_id_type=MESH
        )

    def half(k, j, core):
        return pl.ds(pl.multiple_of((sample_at(y, k) * 2 + j) * 64 + core * 32, 32), 32)

    def b1(k):
        return remote(s1.at[k], r1.at[k], sent.at[k, 0], got_pair.at[k], sib)

    def pair(k):
        for j in range(2):
            s1[k, j] = acc[half(k, j, 1 - c)].astype(BF16)
        b1(k).start()

    def b2(k, d):
        peer = lax.rem(x + d, NX)
        row = pl.multiple_of((peer // 2) * 16, 16)
        col = pl.multiple_of((peer % 2) * STEP, 128)
        return remote(
            xs.at[k, :, pl.ds(row, 16), pl.ds(col, SHARE)], xr.at[k, d - 1],
            sent.at[k, d], got_x.at[k, d - 1], at_x(d, c),
        )

    def along_x(k):
        b1(k).wait_recv()
        for j in range(2):
            xs[k, j] = (acc[half(k, j, c)] + r1[k, j].astype(F32)).astype(BF16)
        for d in (2, 1, 3):
            b2(k, d).start()

    def b3(k, j):
        owner = (p * NY + sample_at(y, k) * 2 + j, lax.axis_index("tensor"))
        return remote(ys.at[k, j], yr.at[y], sent.at[k, 4 + j], got_y.at[y], owner)

    def owners(k):
        return (0, 1) if k < SAMPLES - 1 else (1 - y % 2,)

    def along_y(k):
        for d in range(1, NX):
            b2(k, d).wait_recv()
        total = xs[k, :, pl.ds(my_row, 16), pl.ds(my_col, SHARE)].astype(F32)
        for d in range(NX - 1):
            total = total + xr[k, d].astype(F32)
        ys[k] = total.astype(BF16)
        for j in owners(k):
            b3(k, j).start()

    def b4():
        return remote(zs, zr, sent_all.at[0], got_plane, partner)

    def owned():
        total = ys[SAMPLES - 1, y % 2].astype(F32)
        for d in (4, 3, 5, 2, 6, 1, 7):
            source = lax.rem(y + d, NY)
            remote(ys.at[0, 0], yr.at[source], sent.at[0, 4], got_y.at[source], at_y(d)).wait_recv()
            total = total + yr[source].astype(F32)
        return total

    def planes(more):
        zs[...] = (owned() + more[...].astype(F32)).astype(BF16)
        b4().start()

    def b5(d, other, core, source):
        return remote(
            fs, ar.at[core, source], sent_all.at[d * 2 + other], got_all.at[core, source],
            at_x(d, 1 - c if other else c),
        )

    def spread():
        b4().wait_recv()
        fs[...] = (zs[...].astype(F32) + zr[...].astype(F32)).astype(BF16)
        for d, o in everyone:
            b5(d, o, c, x).start()
        ar[c, x] = fs[...]

    def collect(out):
        for d, o in everyone:
            b5(d, o, 1 - c if o else c, lax.rem(x + d, NX)).wait_recv()
        for core in range(2):
            for i in range(2):
                rows = pl.ds(core * 32 + i * 16, 16)
                out[rows, pl.ds(0, SHARE)] = ar[core, 2 * i]
                out[rows, pl.ds(SHARE, DV - SHARE)] = ar[core, 2 * i + 1, :, pl.ds(SHARE - STEP, DV - SHARE)]

    def shared_sent():
        for k in range(SAMPLES):
            b1(k).wait_send()
            for d in range(1, NX):
                b2(k, d).wait_send()
            for j in owners(k):
                b3(k, j).wait_send()

    def all_sent():
        shared_sent()
        b4().wait_send()
        for d, o in everyone:
            b5(d, o, c, x).wait_send()

    return dict(
        pair=pair, along_x=along_x, along_y=along_y, planes=planes, spread=spread, collect=collect, sent=all_sent,
        owned=owned, shared_sent=shared_sent,
    )


def sample_at(y, k):
    return lax.rem(y // 2 + 1 + k, SAMPLES)


def reduction_bufs():
    shapes = [(SAMPLES, 2, 32, DV)] * 3 + [(SAMPLES, NX - 1, 2, 16, SHARE), (SAMPLES, 2, 16, SHARE)]
    shapes += [(NY, 16, SHARE)] + [(16, SHARE)] * 3 + [(2, NX, 16, SHARE)]
    return [pltpu.VMEM(shape, BF16) for shape in shapes]


def reduction_sems():
    dma = pltpu.SemaphoreType.DMA
    shapes = [(SAMPLES, 6), (8,), (SAMPLES,), (SAMPLES, NX - 1), (NY,)]
    return [dma(shape) for shape in shapes] + [dma, dma((2, NX))]


def kernel(
    gate, visible, vision, wk, wv, query, cot, att_out, vis_out,
    wbuf, xbuf, qbuf, gbuf, abuf, bias, kvbuf, dkv, acc,
    xbuf2, qbuf2, gbuf2, abuf2, bias2, acc2, mine2, more,
    obuf, bufs, bufs2, lsem, lw, lq, lg, lo, zsend, zrecv, xsems, xsems2, msend, mrecv, sems, sems2,
):
    section = lax.axis_index("section")
    tensor = lax.axis_index("tensor")
    p = section // NY
    y = section % NY
    x = tensor // 4
    zh = (tensor // 2) % 2
    c = tensor % 2
    sib = (section, tensor + 1 - 2 * c)

    def at_y(d):
        return (p * NY + lax.rem(y + d, NY), tensor)

    def at_x(d, core):
        return (section, lax.rem(x + d, NX) * 4 + zh * 2 + core)

    partner = (section, x * 4 + (1 - zh) * 2 + c)

    own_x = pltpu.make_async_copy(vision, xbuf.at[pl.ds(y * 64, 64)], lsem.at[0])
    own_x.start()

    def local_w(h, kv):
        ref = wv if kv else wk
        return pltpu.make_async_copy(
            ref.at[:, pl.ds(h * HD, HD)],
            wbuf.at[h, pl.ds(p * QB, QB), pl.ds(kv * HD, HD)],
            lw.at[h, kv],
        )

    for h in range(HEADS):
        local_w(h, 0).start()
        local_w(h, 1).start()

    def local_q(h):
        return pltpu.make_async_copy(query.at[0, :, pl.ds(h * HD, HD)], qbuf.at[h], lq.at[h])

    def local_g(h):
        return pltpu.make_async_copy(cot.at[0, :, pl.ds(h * HD, HD)], gbuf.at[h], lg.at[h])

    for h in range(HEADS):
        local_q(h).start()
        local_g(h).start()

    barrier = pltpu.get_barrier_semaphore()

    def greet(device):
        pl.semaphore_signal(barrier, inc=1, device_id=device, device_id_type=MESH)

    has_left = p > 0
    has_right = p < NZ - 1
    inner = jnp.logical_and(has_left, has_right)
    end = jnp.logical_or(p == 0, p == NZ - 1)
    mate = section + NY - 2 * NY * (p % 2)

    def to_mate(i, src, dst):
        return pltpu.make_async_remote_copy(
            src_ref=src, dst_ref=dst, send_sem=msend.at[i], recv_sem=mrecv.at[i],
            device_id=(mate, tensor), device_id_type=MESH,
        )

    own_half = pl.ds(pl.multiple_of(y * 64 + c * 32, 32), 32)

    def lend(i):
        if i == 0:
            return to_mate(0, xbuf.at[own_half], xbuf2.at[own_half])
        return to_mate(1, qbuf.at[0], qbuf2.at[0]) if i == 1 else to_mate(2, gbuf.at[0], gbuf2.at[0])

    def give_back():
        return to_mate(3, abuf2.at[0], abuf.at[0])

    def give_sum():
        return to_mate(4, mine2, more)

    @pl.when(has_left)
    def _():
        greet((section - NY, tensor))

    @pl.when(has_right)
    def _():
        greet((section + NY, tensor))

    for d in range(1, NY):
        greet(at_y(d))
    for d in range(1, NX):
        greet(at_x(d, c))
    for d in range(NX):
        greet(at_x(d, 1 - c))
    greet(partner)
    ends = jnp.where(has_left, 1, 0) + jnp.where(has_right, 1, 0)
    pl.semaphore_wait(barrier, 15 + ends)

    def zcopy(q, h, right):
        rows = pl.ds(pl.multiple_of(q * QB, 16), QB)
        return pltpu.make_async_remote_copy(
            src_ref=wbuf.at[h, rows],
            dst_ref=wbuf.at[h, rows],
            send_sem=zsend.at[right, q, h],
            recv_sem=zrecv.at[q, h],
            device_id=(section + (NY if right else -NY), tensor),
            device_id_type=MESH,
        )

    def send_left(h):
        return p > (1 if h == 0 else 0)

    def send_right(h):
        return p < (NZ - 2 if h == 0 else NZ - 1)

    for h in range(HEADS):
        local_w(h, 0).wait()
        local_w(h, 1).wait()

        @pl.when(send_left(h))
        def _():
            zcopy(p, h, 0).start()

        @pl.when(send_right(h))
        def _():
            zcopy(p, h, 1).start()

        if h == 0:
            own_x.wait()

            @pl.when(end)
            def _():
                lend(0).start()

        if h == 2:
            local_q(0).wait()
            local_g(0).wait()

            @pl.when(end)
            def _():
                lend(1).start()
                lend(2).start()

    def relay(d, h, takes):
        relay_sides(d, h, takes, takes)

    def relay_sides(d, h, from_right, from_left):
        @pl.when(jnp.logical_and(from_right, p + d < NZ))
        def _():
            q = p + d
            zcopy(q, h, 0).wait_recv()

            @pl.when(send_left(h))
            def _():
                zcopy(q, h, 0).start()

        @pl.when(jnp.logical_and(from_left, p - d >= 0))
        def _():
            q = p - d
            zcopy(q, h, 1).wait_recv()

            @pl.when(send_right(h))
            def _():
                zcopy(q, h, 1).start()

    def xcopy(source, to, core, buf=xbuf, xs=xsems):
        rows = pl.ds(pl.multiple_of(source * 64 + core * 32, 32), 32)
        sent, ring, side = xs
        return pltpu.make_async_remote_copy(
            src_ref=buf.at[rows],
            dst_ref=buf.at[rows],
            send_sem=sent.at[to, source],
            recv_sem=side.at[source] if to == 2 else ring.at[source],
            device_id=(at_y(1), at_y(NY - 1), sib)[to],
            device_id_type=MESH,
        )

    def xcopy2(source, to, core):
        return xcopy(source, to, core, xbuf2, xsems2)

    def step(t, copy):
        below = lax.rem(y + NY - t, NY)
        copy(below, 0, c).wait_recv()
        if t < 4:
            copy(below, 0, c).start()
        copy(below, 2, c).start()
        if t < 4:
            above = lax.rem(y + t, NY)
            copy(above, 1, c).wait_recv()
            if t < 3:
                copy(above, 1, c).start()
            copy(above, 2, c).start()

    def step_sent(t, copy):
        below = lax.rem(y + NY - t, NY)
        if t < 4:
            copy(below, 0, c).wait_send()
        copy(below, 2, c).wait_send()
        if t < 4:
            above = lax.rem(y + t, NY)
            if t < 3:
                copy(above, 1, c).wait_send()
            copy(above, 2, c).wait_send()

    xcopy(y, 0, c).start()
    xcopy(y, 1, c).start()

    lane = lax.broadcasted_iota(jnp.int32, (128, 256), 1)
    image = lax.broadcasted_iota(jnp.int32, (128, 256), 0) // 64
    def mask(micro, s):
        seen = jnp.where(
            lane < 128,
            jnp.where(lane < 64, visible[micro, s, 0], visible[micro, s, 1]),
            jnp.where(lane < 192, visible[micro, s, 2], visible[micro, s, 3]),
        )
        return jnp.where(seen == image, 0.0, -1e30).astype(F32)

    for s in range(SAMPLES):
        bias[s] = mask(p, s)
        bias2[s] = mask(mate // NY, s)
    acc[...] = jnp.zeros_like(acc)

    @pl.when(inner)
    def _():
        more[...] = jnp.zeros_like(more)
        lend(0).wait_recv()
        for to in range(3):
            xcopy2(y, to, c).start()

    for t in range(1, 5):
        step(t, xcopy)

        @pl.when(inner)
        def _():
            step(t, xcopy2)

        if t < 4:
            relay(1, t - 1, inner)
        else:
            relay_sides(1, t - 1, p == 1, p == 2)
        if t > 1:
            relay(1, t - 1, end)
    for t in range(1, NY):
        source = lax.rem(y + t, NY)
        xcopy(source, 2, 1 - c).wait_recv()
    factor = jnp.tanh(jnp.full((1, HD), gate[y], F32))

    own = (qbuf, gbuf, abuf, bias)
    lent = (qbuf2, gbuf2, abuf2, bias2)

    def ready(h):
        for d in range(2, NZ):
            relay(d, h, end)
        local_q(h).wait()
        local_g(h).wait()
        project(h, xbuf)

    def project(h, tokens):
        kvbuf[...] = nn(tokens[...], wbuf[h]).astype(BF16)

    def attend(h, s, arrays=own):
        query_ref, cot_ref, att_ref, bias_ref = arrays
        image_rows = pl.ds(pl.multiple_of(s * 128, 128), 128)
        text_rows = pl.ds(pl.multiple_of(s * 256, 256), 256)
        keys = kvbuf[image_rows, :HD]
        values = kvbuf[image_rows, HD:]
        qs = query_ref[h, text_rows]
        hg = (factor * cot_ref[h, text_rows].astype(F32)).astype(BF16)
        e = jnp.exp(nt(keys, qs) * SCALE + bias_ref[s])
        total = jnp.sum(e, axis=0, keepdims=True)
        probs = e * (1.0 / jnp.where(total > 0.0, total, 1.0))
        probs_b = probs.astype(BF16)
        att_ref[h, text_rows] = (factor * tn(probs_b, values)).astype(BF16)
        dkv[image_rows, HD:] = nn(probs_b, hg).astype(BF16)
        pg = nt(values, hg)
        delta = jnp.sum(probs * pg, axis=0, keepdims=True)
        sg = (probs * (pg - delta) * SCALE).astype(BF16)
        dkv[image_rows, :HD] = nn(sg, qs).astype(BF16)

    def out_copy(h):
        return pltpu.make_async_copy(abuf.at[h], att_out.at[0, :, pl.ds(h * HD, HD)], lo.at[h])

    place, peers = (section, p, y, x, c), (sib, partner, at_y, at_x)
    reduce = reduction(acc, bufs, sems, place, peers)
    reduce2 = reduction(acc2, bufs2, sems2, place, peers)

    relay(2, 0, inner)
    relay(2, 1, inner)

    @pl.when(inner)
    def _():
        for t in range(NY):
            xcopy2(lax.rem(y + t, NY), 2, 1 - c).wait_recv()
        lend(1).wait_recv()
        lend(2).wait_recv()
        project(0, xbuf2)
        for s in range(SAMPLES):
            attend(0, s, lent)
        give_back().start()
        acc2[...] = nt(dkv[...], wbuf[0])
        for k in range(SAMPLES):
            reduce2["pair"](k)

    relay(2, 2, inner)
    relay_sides(1, HEADS - 1, p == 2, p == 1)

    @pl.when(inner)
    def _():
        project(0, xbuf)
        for s in range(SAMPLES):
            attend(0, s)
        out_copy(0).start()
        acc[...] += nt(dkv[...], wbuf[0])

    relay(2, HEADS - 1, inner)

    for h in range(1, HEADS - 1):
        ready(h)
        for s in range(SAMPLES):
            attend(h, s)
        out_copy(h).start()
        acc[...] += nt(dkv[...], wbuf[h])

        @pl.when(inner)
        def _():
            for k in range(SAMPLES):
                reduce2["along_x" if h == 1 else "along_y"](k)

    ready(HEADS - 1)
    for k in range(SAMPLES):
        s = sample_at(y, k)
        attend(HEADS - 1, s)
        rows = pl.ds(pl.multiple_of(s * 128, 128), 128)
        acc[rows] += nt(dkv[rows], wbuf[HEADS - 1])
        reduce["pair"](k)
        if k:
            reduce["along_x"](k - 1)
    reduce["along_x"](SAMPLES - 1)
    out_copy(HEADS - 1).start()

    @pl.when(inner)
    def _():
        mine2[...] = reduce2["owned"]().astype(BF16)
        give_sum().start()

    @pl.when(end)
    def _():
        give_back().wait_recv()
        out_copy(0).start()

    for k in range(SAMPLES):
        reduce["along_y"](k)

    @pl.when(end)
    def _():
        give_sum().wait_recv()

    reduce["planes"](more)
    reduce["spread"]()
    reduce["collect"](obuf)
    last = pltpu.make_async_copy(obuf, vis_out, lsem.at[1])
    last.start()

    for h in range(HEADS):
        for q in range(NZ):
            from_right = jnp.logical_and(send_left(h), p <= q)
            from_left = jnp.logical_and(send_right(h), p >= q)

            @pl.when(from_right)
            def _():
                zcopy(q, h, 0).wait_send()

            @pl.when(from_left)
            def _():
                zcopy(q, h, 1).wait_send()

    xcopy(y, 0, c).wait_send()
    xcopy(y, 1, c).wait_send()
    for t in range(1, 5):
        step_sent(t, xcopy)

    @pl.when(inner)
    def _():
        for to in range(3):
            xcopy2(y, to, c).wait_send()
        for t in range(1, 5):
            step_sent(t, xcopy2)
        give_back().wait_send()
        give_sum().wait_send()
        reduce2["shared_sent"]()

    @pl.when(end)
    def _():
        for i in range(3):
            lend(i).wait_send()

    reduce["sent"]()
    for h in range(HEADS):
        out_copy(h).wait()
    last.wait()


def shards(vision_tokens, key_weight, value_weight, queries, gate, visible, out_grad):
    dma = pltpu.SemaphoreType.DMA
    hbm = pl.BlockSpec(memory_space=pltpu.HBM)
    smem = pl.BlockSpec(memory_space=pltpu.SMEM)
    return pl.pallas_call(
        kernel,
        out_shape=(
            jax.ShapeDtypeStruct(queries.shape, BF16),
            jax.ShapeDtypeStruct(vision_tokens.shape, BF16),
        ),
        in_specs=[smem, smem, hbm, hbm, hbm, hbm, hbm],
        out_specs=(pl.BlockSpec(memory_space=pl.ANY),) * 2,
        scratch_shapes=[
            pltpu.VMEM((HEADS, DV, 2 * HD), BF16),
            pltpu.VMEM((VT, DV), BF16),
            pltpu.VMEM((HEADS, 1024, HD), BF16),
            pltpu.VMEM((HEADS, 1024, HD), BF16),
            pltpu.VMEM((HEADS, 1024, HD), BF16),
            pltpu.VMEM((SAMPLES, 128, 256), F32),
            pltpu.VMEM((VT, 2 * HD), BF16),
            pltpu.VMEM((VT, 2 * HD), BF16),
            pltpu.VMEM((VT, DV), F32),
            pltpu.VMEM((VT, DV), BF16),
            pltpu.VMEM((1, 1024, HD), BF16),
            pltpu.VMEM((1, 1024, HD), BF16),
            pltpu.VMEM((1, 1024, HD), BF16),
            pltpu.VMEM((SAMPLES, 128, 256), F32),
            pltpu.VMEM((VT, DV), F32),
            pltpu.VMEM((16, SHARE), BF16),
            pltpu.VMEM((16, SHARE), BF16),
            pltpu.VMEM((64, DV), BF16),
            reduction_bufs(),
            reduction_bufs(),
            dma((2,)),
            dma((HEADS, 2)),
            dma((HEADS,)),
            dma((HEADS,)),
            dma((HEADS,)),
            dma((2, NZ, HEADS)),
            dma((NZ, HEADS)),
            [dma((3, NY)), dma((NY,)), dma((NY,))],
            [dma((3, NY)), dma((NY,)), dma((NY,))],
            dma((5,)),
            dma((5,)),
            reduction_sems(),
            reduction_sems(),
        ],
        compiler_params=pltpu.CompilerParams(
            collective_id=0, has_side_effects=True, vmem_limit_bytes=60 * 2**20
        ),
        cost_estimate=pl.CostEstimate(flops=4 * 10**9, bytes_accessed=5 * 10**6, transcendentals=2**19),
    )(gate, visible, vision_tokens, key_weight, value_weight, queries, out_grad)


def solution(mesh):
    placed = (
        P("section", None),
        P("section", "tensor"),
        P("section", "tensor"),
        P("section", None, "tensor"),
        P(),
        P(),
        P("section", None, "tensor"),
    )
    return jax.shard_map(
        shards,
        mesh=mesh,
        in_specs=placed,
        out_specs=(P("section", None, "tensor"), P("section", None)),
        check_vma=False,
    )
```

```python
import jax
import jax.numpy as jnp
from jax import lax
from jax.experimental import pallas as pl
from jax.experimental.pallas import tpu as pltpu
from jax.sharding import PartitionSpec as P

HD = 128
NZ, NY, NX = 4, 8, 4
HEADS = 4
SAMPLES = 4
QB = 416
DV = 1664
VT = 512
SHARE = 896
STEP = 768
SCALE = 1.0 / HD**0.5
MESH = pl.DeviceIdType.MESH
F32 = jnp.float32
BF16 = jnp.bfloat16


def nt(a, b):
    return lax.dot_general(a, b, (((1,), (1,)), ((), ())), preferred_element_type=F32)


def nn(a, b):
    return lax.dot_general(a, b, (((1,), (0,)), ((), ())), preferred_element_type=F32)


def tn(a, b):
    return lax.dot_general(a, b, (((0,), (0,)), ((), ())), preferred_element_type=F32)


def reduction(acc, bufs, sems, place, peers):
    s1, r1, xs, xr, ys, yr, zs, zr, fs, ar = bufs
    sent, sent_all, got_pair, got_x, got_y, got_plane, got_all = sems
    section, p, y, x, c = place
    sib, partner, at_y, at_x = peers
    everyone = [(d, o) for d in (2, 1, 3, 0) for o in (0, 1) if (d, o) != (0, 0)]
    my_row = pl.multiple_of((x // 2) * 16, 16)
    my_col = pl.multiple_of((x % 2) * STEP, 128)

    def remote(src, dst, send, recv, device):
        return pltpu.make_async_remote_copy(
            src_ref=src, dst_ref=dst, send_sem=send, recv_sem=recv, device_id=device, device_id_type=MESH
        )

    def half(k, j, core):
        return pl.ds(pl.multiple_of((sample_at(y, k) * 2 + j) * 64 + core * 32, 32), 32)

    def b1(k):
        return remote(s1.at[k], r1.at[k], sent.at[k, 0], got_pair.at[k], sib)

    def pair(k):
        for j in range(2):
            s1[k, j] = acc[half(k, j, 1 - c)].astype(BF16)
        b1(k).start()

    def b2(k, d):
        peer = lax.rem(x + d, NX)
        row = pl.multiple_of((peer // 2) * 16, 16)
        col = pl.multiple_of((peer % 2) * STEP, 128)
        return remote(
            xs.at[k, :, pl.ds(row, 16), pl.ds(col, SHARE)], xr.at[k, d - 1],
            sent.at[k, d], got_x.at[k, d - 1], at_x(d, c),
        )

    def along_x(k):
        b1(k).wait_recv()
        for j in range(2):
            xs[k, j] = (acc[half(k, j, c)] + r1[k, j].astype(F32)).astype(BF16)
        for d in (2, 1, 3):
            b2(k, d).start()

    def b3(k, j):
        owner = (p * NY + sample_at(y, k) * 2 + j, lax.axis_index("tensor"))
        return remote(ys.at[k, j], yr.at[y], sent.at[k, 4 + j], got_y.at[y], owner)

    def owners(k):
        return (0, 1) if k < SAMPLES - 1 else (1 - y % 2,)

    def along_y(k):
        for d in range(1, NX):
            b2(k, d).wait_recv()
        total = xs[k, :, pl.ds(my_row, 16), pl.ds(my_col, SHARE)].astype(F32)
        for d in range(NX - 1):
            total = total + xr[k, d].astype(F32)
        ys[k] = total.astype(BF16)
        for j in owners(k):
            b3(k, j).start()

    def b4():
        return remote(zs, zr, sent_all.at[0], got_plane, partner)

    def owned():
        total = ys[SAMPLES - 1, y % 2].astype(F32)
        for d in (4, 3, 5, 2, 6, 1, 7):
            source = lax.rem(y + d, NY)
            remote(ys.at[0, 0], yr.at[source], sent.at[0, 4], got_y.at[source], at_y(d)).wait_recv()
            total = total + yr[source].astype(F32)
        return total

    def planes(more):
        zs[...] = (owned() + more[...].astype(F32)).astype(BF16)
        b4().start()

    def b5(d, other, core, source):
        return remote(
            fs, ar.at[core, source], sent_all.at[d * 2 + other], got_all.at[core, source],
            at_x(d, 1 - c if other else c),
        )

    def spread():
        b4().wait_recv()
        fs[...] = (zs[...].astype(F32) + zr[...].astype(F32)).astype(BF16)
        for d, o in everyone:
            b5(d, o, c, x).start()
        ar[c, x] = fs[...]

    def collect(out):
        for d, o in everyone:
            b5(d, o, 1 - c if o else c, lax.rem(x + d, NX)).wait_recv()
        for core in range(2):
            for i in range(2):
                rows = pl.ds(core * 32 + i * 16, 16)
                out[rows, pl.ds(0, SHARE)] = ar[core, 2 * i]
                out[rows, pl.ds(SHARE, DV - SHARE)] = ar[core, 2 * i + 1, :, pl.ds(SHARE - STEP, DV - SHARE)]

    def shared_sent():
        for k in range(SAMPLES):
            b1(k).wait_send()
            for d in range(1, NX):
                b2(k, d).wait_send()
            for j in owners(k):
                b3(k, j).wait_send()

    def all_sent():
        shared_sent()
        b4().wait_send()
        for d, o in everyone:
            b5(d, o, c, x).wait_send()

    return dict(
        pair=pair, along_x=along_x, along_y=along_y, planes=planes, spread=spread, collect=collect, sent=all_sent,
        owned=owned, shared_sent=shared_sent,
    )


def sample_at(y, k):
    return lax.rem(y // 2 + 1 + k, SAMPLES)


def reduction_bufs():
    shapes = [(SAMPLES, 2, 32, DV)] * 3 + [(SAMPLES, NX - 1, 2, 16, SHARE), (SAMPLES, 2, 16, SHARE)]
    shapes += [(NY, 16, SHARE)] + [(16, SHARE)] * 3 + [(2, NX, 16, SHARE)]
    return [pltpu.VMEM(shape, BF16) for shape in shapes]


def reduction_sems():
    dma = pltpu.SemaphoreType.DMA
    shapes = [(SAMPLES, 6), (8,), (SAMPLES,), (SAMPLES, NX - 1), (NY,)]
    return [dma(shape) for shape in shapes] + [dma, dma((2, NX))]


def kernel(
    gate, visible, vision, wk, wv, query, cot, att_out, vis_out,
    wbuf, xbuf, qbuf, gbuf, abuf, bias, kvbuf, dkv, acc,
    xbuf2, qbuf2, gbuf2, abuf2, bias2, acc2, mine2, more,
    obuf, bufs, bufs2, lsem, lw, lq, lg, lo, zsend, zrecv, xsems, xsems2, msend, mrecv, sems, sems2,
):
    section = lax.axis_index("section")
    tensor = lax.axis_index("tensor")
    p = section // NY
    y = section % NY
    x = tensor // 4
    zh = (tensor // 2) % 2
    c = tensor % 2
    sib = (section, tensor + 1 - 2 * c)

    def at_y(d):
        return (p * NY + lax.rem(y + d, NY), tensor)

    def at_x(d, core):
        return (section, lax.rem(x + d, NX) * 4 + zh * 2 + core)

    partner = (section, x * 4 + (1 - zh) * 2 + c)

    own_x = pltpu.make_async_copy(vision, xbuf.at[pl.ds(y * 64, 64)], lsem.at[0])
    own_x.start()

    def local_w(h, kv):
        ref = wv if kv else wk
        return pltpu.make_async_copy(
            ref.at[:, pl.ds(h * HD, HD)],
            wbuf.at[h, pl.ds(p * QB, QB), pl.ds(kv * HD, HD)],
            lw.at[h, kv],
        )

    for h in range(HEADS):
        local_w(h, 0).start()
        local_w(h, 1).start()

    def local_q(h):
        return pltpu.make_async_copy(query.at[0, :, pl.ds(h * HD, HD)], qbuf.at[h], lq.at[h])

    def local_g(h):
        return pltpu.make_async_copy(cot.at[0, :, pl.ds(h * HD, HD)], gbuf.at[h], lg.at[h])

    for h in range(HEADS):
        local_q(h).start()
        local_g(h).start()

    barrier = pltpu.get_barrier_semaphore()

    def greet(device):
        pl.semaphore_signal(barrier, inc=1, device_id=device, device_id_type=MESH)

    has_left = p > 0
    has_right = p < NZ - 1
    inner = jnp.logical_and(has_left, has_right)
    end = jnp.logical_or(p == 0, p == NZ - 1)
    mate = section + NY - 2 * NY * (p % 2)

    def to_mate(i, src, dst):
        return pltpu.make_async_remote_copy(
            src_ref=src, dst_ref=dst, send_sem=msend.at[i], recv_sem=mrecv.at[i],
            device_id=(mate, tensor), device_id_type=MESH,
        )

    own_half = pl.ds(pl.multiple_of(y * 64 + c * 32, 32), 32)

    def lend(i):
        if i == 0:
            return to_mate(0, xbuf.at[own_half], xbuf2.at[own_half])
        return to_mate(1, qbuf.at[0], qbuf2.at[0]) if i == 1 else to_mate(2, gbuf.at[0], gbuf2.at[0])

    def give_back():
        return to_mate(3, abuf2.at[0], abuf.at[0])

    def give_sum():
        return to_mate(4, mine2, more)

    @pl.when(has_left)
    def _():
        greet((section - NY, tensor))

    @pl.when(has_right)
    def _():
        greet((section + NY, tensor))

    for d in range(1, NY):
        greet(at_y(d))
    for d in range(1, NX):
        greet(at_x(d, c))
    for d in range(NX):
        greet(at_x(d, 1 - c))
    greet(partner)
    ends = jnp.where(has_left, 1, 0) + jnp.where(has_right, 1, 0)
    pl.semaphore_wait(barrier, 15 + ends)

    def zcopy(q, h, right):
        rows = pl.ds(pl.multiple_of(q * QB, 16), QB)
        return pltpu.make_async_remote_copy(
            src_ref=wbuf.at[h, rows],
            dst_ref=wbuf.at[h, rows],
            send_sem=zsend.at[right, q, h],
            recv_sem=zrecv.at[q, h],
            device_id=(section + (NY if right else -NY), tensor),
            device_id_type=MESH,
        )

    def send_left(h):
        return p > (1 if h == 0 else 0)

    def send_right(h):
        return p < (NZ - 2 if h == 0 else NZ - 1)

    for h in range(HEADS):
        local_w(h, 0).wait()
        local_w(h, 1).wait()

        @pl.when(send_left(h))
        def _():
            zcopy(p, h, 0).start()

        @pl.when(send_right(h))
        def _():
            zcopy(p, h, 1).start()

        if h == 0:
            own_x.wait()

            @pl.when(end)
            def _():
                lend(0).start()

        if h == 2:
            local_q(0).wait()
            local_g(0).wait()

            @pl.when(end)
            def _():
                lend(1).start()
                lend(2).start()

    def relay(d, h, takes):
        relay_sides(d, h, takes, takes)

    def relay_sides(d, h, from_right, from_left):
        @pl.when(jnp.logical_and(from_right, p + d < NZ))
        def _():
            q = p + d
            zcopy(q, h, 0).wait_recv()

            @pl.when(send_left(h))
            def _():
                zcopy(q, h, 0).start()

        @pl.when(jnp.logical_and(from_left, p - d >= 0))
        def _():
            q = p - d
            zcopy(q, h, 1).wait_recv()

            @pl.when(send_right(h))
            def _():
                zcopy(q, h, 1).start()

    def xcopy(source, to, core, buf=xbuf, xs=xsems):
        rows = pl.ds(pl.multiple_of(source * 64 + core * 32, 32), 32)
        sent, ring, side = xs
        return pltpu.make_async_remote_copy(
            src_ref=buf.at[rows],
            dst_ref=buf.at[rows],
            send_sem=sent.at[to, source],
            recv_sem=side.at[source] if to == 2 else ring.at[source],
            device_id=(at_y(1), at_y(NY - 1), sib)[to],
            device_id_type=MESH,
        )

    def xcopy2(source, to, core):
        return xcopy(source, to, core, xbuf2, xsems2)

    def step(t, copy):
        below = lax.rem(y + NY - t, NY)
        copy(below, 0, c).wait_recv()
        if t < 4:
            copy(below, 0, c).start()
        copy(below, 2, c).start()
        if t < 4:
            above = lax.rem(y + t, NY)
            copy(above, 1, c).wait_recv()
            if t < 3:
                copy(above, 1, c).start()
            copy(above, 2, c).start()

    def step_sent(t, copy):
        below = lax.rem(y + NY - t, NY)
        if t < 4:
            copy(below, 0, c).wait_send()
        copy(below, 2, c).wait_send()
        if t < 4:
            above = lax.rem(y + t, NY)
            if t < 3:
                copy(above, 1, c).wait_send()
            copy(above, 2, c).wait_send()

    xcopy(y, 0, c).start()
    xcopy(y, 1, c).start()

    lane = lax.broadcasted_iota(jnp.int32, (128, 256), 1)
    image = lax.broadcasted_iota(jnp.int32, (128, 256), 0) // 64
    def mask(micro, s):
        seen = jnp.where(
            lane < 128,
            jnp.where(lane < 64, visible[micro, s, 0], visible[micro, s, 1]),
            jnp.where(lane < 192, visible[micro, s, 2], visible[micro, s, 3]),
        )
        return jnp.where(seen == image, 0.0, -1e30).astype(F32)

    for s in range(SAMPLES):
        bias[s] = mask(p, s)
        bias2[s] = mask(mate // NY, s)
    acc[...] = jnp.zeros_like(acc)

    @pl.when(inner)
    def _():
        more[...] = jnp.zeros_like(more)
        lend(0).wait_recv()
        for to in range(3):
            xcopy2(y, to, c).start()

    for t in range(1, 5):
        step(t, xcopy)
        if t < 4:
            relay(1, t - 1, inner)
        else:
            relay_sides(1, t - 1, p == 1, p == 2)

        @pl.when(inner)
        def _():
            step(t, xcopy2)

        if t > 1:
            relay(1, t - 1, end)
    for t in range(1, NY):
        source = lax.rem(y + t, NY)
        xcopy(source, 2, 1 - c).wait_recv()
    factor = jnp.tanh(jnp.full((1, HD), gate[y], F32))

    own = (qbuf, gbuf, abuf, bias)
    lent = (qbuf2, gbuf2, abuf2, bias2)

    def ready(h):
        for d in range(2, NZ):
            relay(d, h, end)
        local_q(h).wait()
        local_g(h).wait()
        project(h, xbuf)

    def project(h, tokens):
        kvbuf[...] = nn(tokens[...], wbuf[h]).astype(BF16)

    def attend(h, s, arrays=own):
        query_ref, cot_ref, att_ref, bias_ref = arrays
        image_rows = pl.ds(pl.multiple_of(s * 128, 128), 128)
        text_rows = pl.ds(pl.multiple_of(s * 256, 256), 256)
        keys = kvbuf[image_rows, :HD]
        values = kvbuf[image_rows, HD:]
        qs = query_ref[h, text_rows]
        hg = (factor * cot_ref[h, text_rows].astype(F32)).astype(BF16)
        e = jnp.exp(nt(keys, qs) * SCALE + bias_ref[s])
        total = jnp.sum(e, axis=0, keepdims=True)
        probs = e * (1.0 / jnp.where(total > 0.0, total, 1.0))
        probs_b = probs.astype(BF16)
        att_ref[h, text_rows] = (factor * tn(probs_b, values)).astype(BF16)
        dkv[image_rows, HD:] = nn(probs_b, hg).astype(BF16)
        pg = nt(values, hg)
        delta = jnp.sum(probs * pg, axis=0, keepdims=True)
        sg = (probs * (pg - delta) * SCALE).astype(BF16)
        dkv[image_rows, :HD] = nn(sg, qs).astype(BF16)

    def out_copy(h):
        return pltpu.make_async_copy(abuf.at[h], att_out.at[0, :, pl.ds(h * HD, HD)], lo.at[h])

    place, peers = (section, p, y, x, c), (sib, partner, at_y, at_x)
    reduce = reduction(acc, bufs, sems, place, peers)
    reduce2 = reduction(acc2, bufs2, sems2, place, peers)

    relay(2, 0, inner)
    relay(2, 1, inner)

    @pl.when(inner)
    def _():
        for t in range(NY):
            xcopy2(lax.rem(y + t, NY), 2, 1 - c).wait_recv()
        lend(1).wait_recv()
        lend(2).wait_recv()
        project(0, xbuf2)
        for s in range(SAMPLES):
            attend(0, s, lent)
        give_back().start()
        acc2[...] = nt(dkv[...], wbuf[0])
        for k in range(SAMPLES):
            reduce2["pair"](k)

    relay(2, 2, inner)
    relay_sides(1, HEADS - 1, p == 2, p == 1)

    @pl.when(inner)
    def _():
        for k in range(SAMPLES):
            reduce2["along_x"](k)
        project(0, xbuf)
        for s in range(SAMPLES):
            attend(0, s)
        out_copy(0).start()
        acc[...] += nt(dkv[...], wbuf[0])

    relay(2, HEADS - 1, inner)

    for h in range(1, HEADS - 1):
        ready(h)
        for s in range(SAMPLES):
            attend(h, s)
        out_copy(h).start()
        acc[...] += nt(dkv[...], wbuf[h])

        if h == HEADS - 2:

            @pl.when(inner)
            def _():
                for k in range(SAMPLES):
                    reduce2["along_y"](k)

    ready(HEADS - 1)
    for k in range(SAMPLES):
        s = sample_at(y, k)
        attend(HEADS - 1, s)
        rows = pl.ds(pl.multiple_of(s * 128, 128), 128)
        acc[rows] += nt(dkv[rows], wbuf[HEADS - 1])
        reduce["pair"](k)
        if k:
            reduce["along_x"](k - 1)
    reduce["along_x"](SAMPLES - 1)
    out_copy(HEADS - 1).start()

    @pl.when(inner)
    def _():
        mine2[...] = reduce2["owned"]().astype(BF16)
        give_sum().start()

    @pl.when(end)
    def _():
        give_back().wait_recv()
        out_copy(0).start()

    for k in range(SAMPLES):
        reduce["along_y"](k)

    @pl.when(end)
    def _():
        give_sum().wait_recv()

    reduce["planes"](more)
    reduce["spread"]()
    reduce["collect"](obuf)
    last = pltpu.make_async_copy(obuf, vis_out, lsem.at[1])
    last.start()

    for h in range(HEADS):
        for q in range(NZ):
            from_right = jnp.logical_and(send_left(h), p <= q)
            from_left = jnp.logical_and(send_right(h), p >= q)

            @pl.when(from_right)
            def _():
                zcopy(q, h, 0).wait_send()

            @pl.when(from_left)
            def _():
                zcopy(q, h, 1).wait_send()

    xcopy(y, 0, c).wait_send()
    xcopy(y, 1, c).wait_send()
    for t in range(1, 5):
        step_sent(t, xcopy)

    @pl.when(inner)
    def _():
        for to in range(3):
            xcopy2(y, to, c).wait_send()
        for t in range(1, 5):
            step_sent(t, xcopy2)
        give_back().wait_send()
        give_sum().wait_send()
        reduce2["shared_sent"]()

    @pl.when(end)
    def _():
        for i in range(3):
            lend(i).wait_send()

    reduce["sent"]()
    for h in range(HEADS):
        out_copy(h).wait()
    last.wait()


def shards(vision_tokens, key_weight, value_weight, queries, gate, visible, out_grad):
    dma = pltpu.SemaphoreType.DMA
    hbm = pl.BlockSpec(memory_space=pltpu.HBM)
    smem = pl.BlockSpec(memory_space=pltpu.SMEM)
    return pl.pallas_call(
        kernel,
        out_shape=(
            jax.ShapeDtypeStruct(queries.shape, BF16),
            jax.ShapeDtypeStruct(vision_tokens.shape, BF16),
        ),
        in_specs=[smem, smem, hbm, hbm, hbm, hbm, hbm],
        out_specs=(pl.BlockSpec(memory_space=pl.ANY),) * 2,
        scratch_shapes=[
            pltpu.VMEM((HEADS, DV, 2 * HD), BF16),
            pltpu.VMEM((VT, DV), BF16),
            pltpu.VMEM((HEADS, 1024, HD), BF16),
            pltpu.VMEM((HEADS, 1024, HD), BF16),
            pltpu.VMEM((HEADS, 1024, HD), BF16),
            pltpu.VMEM((SAMPLES, 128, 256), F32),
            pltpu.VMEM((VT, 2 * HD), BF16),
            pltpu.VMEM((VT, 2 * HD), BF16),
            pltpu.VMEM((VT, DV), F32),
            pltpu.VMEM((VT, DV), BF16),
            pltpu.VMEM((1, 1024, HD), BF16),
            pltpu.VMEM((1, 1024, HD), BF16),
            pltpu.VMEM((1, 1024, HD), BF16),
            pltpu.VMEM((SAMPLES, 128, 256), F32),
            pltpu.VMEM((VT, DV), F32),
            pltpu.VMEM((16, SHARE), BF16),
            pltpu.VMEM((16, SHARE), BF16),
            pltpu.VMEM((64, DV), BF16),
            reduction_bufs(),
            reduction_bufs(),
            dma((2,)),
            dma((HEADS, 2)),
            dma((HEADS,)),
            dma((HEADS,)),
            dma((HEADS,)),
            dma((2, NZ, HEADS)),
            dma((NZ, HEADS)),
            [dma((3, NY)), dma((NY,)), dma((NY,))],
            [dma((3, NY)), dma((NY,)), dma((NY,))],
            dma((5,)),
            dma((5,)),
            reduction_sems(),
            reduction_sems(),
        ],
        compiler_params=pltpu.CompilerParams(
            collective_id=0, has_side_effects=True, vmem_limit_bytes=60 * 2**20
        ),
        cost_estimate=pl.CostEstimate(flops=4 * 10**9, bytes_accessed=5 * 10**6, transcendentals=2**19),
    )(gate, visible, vision_tokens, key_weight, value_weight, queries, out_grad)


def solution(mesh):
    placed = (
        P("section", None),
        P("section", "tensor"),
        P("section", "tensor"),
        P("section", None, "tensor"),
        P(),
        P(),
        P("section", None, "tensor"),
    )
    return jax.shard_map(
        shards,
        mesh=mesh,
        in_specs=placed,
        out_specs=(P("section", None, "tensor"), P("section", None)),
        check_vma=False,
    )
```

```python
import jax
import jax.numpy as jnp
from jax import lax
from jax.experimental import pallas as pl
from jax.experimental.pallas import tpu as pltpu
from jax.sharding import PartitionSpec as P

HD = 128
NZ, NY, NX = 4, 8, 4
HEADS = 4
SAMPLES = 4
QB = 416
DV = 1664
VT = 512
SHARE = 896
STEP = 768
SCALE = 1.0 / HD**0.5
MESH = pl.DeviceIdType.MESH
F32 = jnp.float32
BF16 = jnp.bfloat16


def nt(a, b):
    return lax.dot_general(a, b, (((1,), (1,)), ((), ())), preferred_element_type=F32)


def nn(a, b):
    return lax.dot_general(a, b, (((1,), (0,)), ((), ())), preferred_element_type=F32)


def tn(a, b):
    return lax.dot_general(a, b, (((0,), (0,)), ((), ())), preferred_element_type=F32)


def reduction(acc, bufs, sems, place, peers):
    s1, r1, xs, xr, ys, yr, zs, zr, fs, ar = bufs
    sent, sent_all, got_pair, got_x, got_y, got_plane, got_all = sems
    section, p, y, x, c = place
    sib, partner, at_y, at_x = peers
    everyone = [(d, o) for d in (2, 1, 3, 0) for o in (0, 1) if (d, o) != (0, 0)]
    my_row = pl.multiple_of((x // 2) * 16, 16)
    my_col = pl.multiple_of((x % 2) * STEP, 128)

    def remote(src, dst, send, recv, device):
        return pltpu.make_async_remote_copy(
            src_ref=src, dst_ref=dst, send_sem=send, recv_sem=recv, device_id=device, device_id_type=MESH
        )

    def half(k, j, core):
        return pl.ds(pl.multiple_of((sample_at(y, k) * 2 + j) * 64 + core * 32, 32), 32)

    def b1(k):
        return remote(s1.at[k], r1.at[k], sent.at[k, 0], got_pair.at[k], sib)

    def pair(k):
        for j in range(2):
            s1[k, j] = acc[half(k, j, 1 - c)].astype(BF16)
        b1(k).start()

    def b2(k, d):
        peer = lax.rem(x + d, NX)
        row = pl.multiple_of((peer // 2) * 16, 16)
        col = pl.multiple_of((peer % 2) * STEP, 128)
        return remote(
            xs.at[k, :, pl.ds(row, 16), pl.ds(col, SHARE)], xr.at[k, d - 1],
            sent.at[k, d], got_x.at[k, d - 1], at_x(d, c),
        )

    def along_x(k):
        b1(k).wait_recv()
        for j in range(2):
            xs[k, j] = (acc[half(k, j, c)] + r1[k, j].astype(F32)).astype(BF16)
        for d in (2, 1, 3):
            b2(k, d).start()

    def b3(k, j):
        owner = (p * NY + sample_at(y, k) * 2 + j, lax.axis_index("tensor"))
        return remote(ys.at[k, j], yr.at[y], sent.at[k, 4 + j], got_y.at[y], owner)

    def owners(k):
        return (0, 1) if k < SAMPLES - 1 else (1 - y % 2,)

    def along_y(k):
        for d in range(1, NX):
            b2(k, d).wait_recv()
        total = xs[k, :, pl.ds(my_row, 16), pl.ds(my_col, SHARE)].astype(F32)
        for d in range(NX - 1):
            total = total + xr[k, d].astype(F32)
        ys[k] = total.astype(BF16)
        for j in owners(k):
            b3(k, j).start()

    def b4():
        return remote(zs, zr, sent_all.at[0], got_plane, partner)

    def owned():
        total = ys[SAMPLES - 1, y % 2].astype(F32)
        for d in (4, 3, 5, 2, 6, 1, 7):
            source = lax.rem(y + d, NY)
            remote(ys.at[0, 0], yr.at[source], sent.at[0, 4], got_y.at[source], at_y(d)).wait_recv()
            total = total + yr[source].astype(F32)
        return total

    def planes(more):
        zs[...] = (owned() + more[...].astype(F32)).astype(BF16)
        b4().start()

    def b5(d, other, core, source):
        return remote(
            fs, ar.at[core, source], sent_all.at[d * 2 + other], got_all.at[core, source],
            at_x(d, 1 - c if other else c),
        )

    def spread():
        b4().wait_recv()
        fs[...] = (zs[...].astype(F32) + zr[...].astype(F32)).astype(BF16)
        for d, o in everyone:
            b5(d, o, c, x).start()
        ar[c, x] = fs[...]

    def collect(out):
        for d, o in everyone:
            b5(d, o, 1 - c if o else c, lax.rem(x + d, NX)).wait_recv()
        for core in range(2):
            for i in range(2):
                rows = pl.ds(core * 32 + i * 16, 16)
                out[rows, pl.ds(0, SHARE)] = ar[core, 2 * i]
                out[rows, pl.ds(SHARE, DV - SHARE)] = ar[core, 2 * i + 1, :, pl.ds(SHARE - STEP, DV - SHARE)]

    def shared_sent():
        for k in range(SAMPLES):
            b1(k).wait_send()
            for d in range(1, NX):
                b2(k, d).wait_send()
            for j in owners(k):
                b3(k, j).wait_send()

    def all_sent():
        shared_sent()
        b4().wait_send()
        for d, o in everyone:
            b5(d, o, c, x).wait_send()

    return dict(
        pair=pair, along_x=along_x, along_y=along_y, planes=planes, spread=spread, collect=collect, sent=all_sent,
        owned=owned, shared_sent=shared_sent,
    )


def sample_at(y, k):
    return lax.rem(y // 2 + 1 + k, SAMPLES)


def reduction_bufs():
    shapes = [(SAMPLES, 2, 32, DV)] * 3 + [(SAMPLES, NX - 1, 2, 16, SHARE), (SAMPLES, 2, 16, SHARE)]
    shapes += [(NY, 16, SHARE)] + [(16, SHARE)] * 3 + [(2, NX, 16, SHARE)]
    return [pltpu.VMEM(shape, BF16) for shape in shapes]


def reduction_sems():
    dma = pltpu.SemaphoreType.DMA
    shapes = [(SAMPLES, 6), (8,), (SAMPLES,), (SAMPLES, NX - 1), (NY,)]
    return [dma(shape) for shape in shapes] + [dma, dma((2, NX))]


def kernel(
    gate, visible, vision, wk, wv, query, cot, att_out, vis_out,
    wbuf, xbuf, qbuf, gbuf, abuf, bias, kvbuf, dkv, acc,
    xbuf2, qbuf2, gbuf2, abuf2, bias2, acc2, mine2, more,
    obuf, bufs, bufs2, lsem, lw, lq, lg, lo, zsend, zrecv, xsems, xsems2, msend, mrecv, sems, sems2,
):
    section = lax.axis_index("section")
    tensor = lax.axis_index("tensor")
    p = section // NY
    y = section % NY
    x = tensor // 4
    zh = (tensor // 2) % 2
    c = tensor % 2
    sib = (section, tensor + 1 - 2 * c)

    def at_y(d):
        return (p * NY + lax.rem(y + d, NY), tensor)

    def at_x(d, core):
        return (section, lax.rem(x + d, NX) * 4 + zh * 2 + core)

    partner = (section, x * 4 + (1 - zh) * 2 + c)

    own_x = pltpu.make_async_copy(vision, xbuf.at[pl.ds(y * 64, 64)], lsem.at[0])
    own_x.start()

    def local_w(h, kv):
        ref = wv if kv else wk
        return pltpu.make_async_copy(
            ref.at[:, pl.ds(h * HD, HD)],
            wbuf.at[h, pl.ds(p * QB, QB), pl.ds(kv * HD, HD)],
            lw.at[h, kv],
        )

    for h in range(HEADS):
        local_w(h, 0).start()
        local_w(h, 1).start()

    def local_q(h):
        return pltpu.make_async_copy(query.at[0, :, pl.ds(h * HD, HD)], qbuf.at[h], lq.at[h])

    def local_g(h):
        return pltpu.make_async_copy(cot.at[0, :, pl.ds(h * HD, HD)], gbuf.at[h], lg.at[h])

    for h in range(HEADS):
        local_q(h).start()
        local_g(h).start()

    barrier = pltpu.get_barrier_semaphore()

    def greet(device):
        pl.semaphore_signal(barrier, inc=1, device_id=device, device_id_type=MESH)

    has_left = p > 0
    has_right = p < NZ - 1
    inner = jnp.logical_and(has_left, has_right)
    end = jnp.logical_or(p == 0, p == NZ - 1)
    mate = section + NY - 2 * NY * (p % 2)

    def to_mate(i, src, dst):
        return pltpu.make_async_remote_copy(
            src_ref=src, dst_ref=dst, send_sem=msend.at[i], recv_sem=mrecv.at[i],
            device_id=(mate, tensor), device_id_type=MESH,
        )

    own_half = pl.ds(pl.multiple_of(y * 64 + c * 32, 32), 32)

    def lend(i):
        if i == 0:
            return to_mate(0, xbuf.at[own_half], xbuf2.at[own_half])
        return to_mate(1, qbuf.at[0], qbuf2.at[0]) if i == 1 else to_mate(2, gbuf.at[0], gbuf2.at[0])

    def give_back():
        return to_mate(3, abuf2.at[0], abuf.at[0])

    def give_sum():
        return to_mate(4, mine2, more)

    @pl.when(has_left)
    def _():
        greet((section - NY, tensor))

    @pl.when(has_right)
    def _():
        greet((section + NY, tensor))

    for d in range(1, NY):
        greet(at_y(d))
    for d in range(1, NX):
        greet(at_x(d, c))
    for d in range(NX):
        greet(at_x(d, 1 - c))
    greet(partner)
    ends = jnp.where(has_left, 1, 0) + jnp.where(has_right, 1, 0)
    pl.semaphore_wait(barrier, 15 + ends)

    def zcopy(q, h, right):
        rows = pl.ds(pl.multiple_of(q * QB, 16), QB)
        return pltpu.make_async_remote_copy(
            src_ref=wbuf.at[h, rows],
            dst_ref=wbuf.at[h, rows],
            send_sem=zsend.at[right, q, h],
            recv_sem=zrecv.at[q, h],
            device_id=(section + (NY if right else -NY), tensor),
            device_id_type=MESH,
        )

    def send_left(h):
        return p > (1 if h == 0 else 0)

    def send_right(h):
        return p < (NZ - 2 if h == 0 else NZ - 1)

    for h in range(HEADS):
        local_w(h, 0).wait()
        local_w(h, 1).wait()

        @pl.when(send_left(h))
        def _():
            zcopy(p, h, 0).start()

        @pl.when(send_right(h))
        def _():
            zcopy(p, h, 1).start()

        if h == 0:
            own_x.wait()

            @pl.when(end)
            def _():
                lend(0).start()

        if h == 2:
            local_q(0).wait()
            local_g(0).wait()

            @pl.when(end)
            def _():
                lend(1).start()
                lend(2).start()

    def relay(d, h, takes):
        relay_sides(d, h, takes, takes)

    def relay_sides(d, h, from_right, from_left):
        @pl.when(jnp.logical_and(from_right, p + d < NZ))
        def _():
            q = p + d
            zcopy(q, h, 0).wait_recv()

            @pl.when(send_left(h))
            def _():
                zcopy(q, h, 0).start()

        @pl.when(jnp.logical_and(from_left, p - d >= 0))
        def _():
            q = p - d
            zcopy(q, h, 1).wait_recv()

            @pl.when(send_right(h))
            def _():
                zcopy(q, h, 1).start()

    def xcopy(source, to, core, buf=xbuf, xs=xsems):
        rows = pl.ds(pl.multiple_of(source * 64 + core * 32, 32), 32)
        sent, ring, side = xs
        return pltpu.make_async_remote_copy(
            src_ref=buf.at[rows],
            dst_ref=buf.at[rows],
            send_sem=sent.at[to, source],
            recv_sem=side.at[source] if to == 2 else ring.at[source],
            device_id=(at_y(1), at_y(NY - 1), sib)[to],
            device_id_type=MESH,
        )

    def xcopy2(source, to, core):
        return xcopy(source, to, core, xbuf2, xsems2)

    def step(t, copy):
        below = lax.rem(y + NY - t, NY)
        copy(below, 0, c).wait_recv()
        if t < 4:
            copy(below, 0, c).start()
        copy(below, 2, c).start()
        if t < 4:
            above = lax.rem(y + t, NY)
            copy(above, 1, c).wait_recv()
            if t < 3:
                copy(above, 1, c).start()
            copy(above, 2, c).start()

    def step_sent(t, copy):
        below = lax.rem(y + NY - t, NY)
        if t < 4:
            copy(below, 0, c).wait_send()
        copy(below, 2, c).wait_send()
        if t < 4:
            above = lax.rem(y + t, NY)
            if t < 3:
                copy(above, 1, c).wait_send()
            copy(above, 2, c).wait_send()

    xcopy(y, 0, c).start()
    xcopy(y, 1, c).start()

    lane = lax.broadcasted_iota(jnp.int32, (128, 256), 1)
    image = lax.broadcasted_iota(jnp.int32, (128, 256), 0) // 64
    def mask(micro, s):
        seen = jnp.where(
            lane < 128,
            jnp.where(lane < 64, visible[micro, s, 0], visible[micro, s, 1]),
            jnp.where(lane < 192, visible[micro, s, 2], visible[micro, s, 3]),
        )
        return jnp.where(seen == image, 0.0, -1e30).astype(F32)

    for s in range(SAMPLES):
        bias[s] = mask(p, s)
        bias2[s] = mask(mate // NY, s)
    acc[...] = jnp.zeros_like(acc)

    @pl.when(inner)
    def _():
        more[...] = jnp.zeros_like(more)
        lend(0).wait_recv()
        for to in range(3):
            xcopy2(y, to, c).start()

    for t in range(1, 5):
        step(t, xcopy)
        if t < 4:
            relay(1, t - 1, inner)
        else:
            relay_sides(1, t - 1, p == 1, p == 2)

        @pl.when(inner)
        def _():
            step(t, xcopy2)

        if t > 1:
            relay(1, t - 1, end)
    for t in range(1, NY):
        source = lax.rem(y + t, NY)
        xcopy(source, 2, 1 - c).wait_recv()
    factor = jnp.tanh(jnp.full((1, HD), gate[y], F32))

    own = (qbuf, gbuf, abuf, bias)
    lent = (qbuf2, gbuf2, abuf2, bias2)

    def ready(h):
        for d in range(2, NZ):
            relay(d, h, end)
        local_q(h).wait()
        local_g(h).wait()
        project(h, xbuf)

    def project(h, tokens):
        kvbuf[...] = nn(tokens[...], wbuf[h]).astype(BF16)

    def attend(h, s, arrays=own):
        query_ref, cot_ref, att_ref, bias_ref = arrays
        image_rows = pl.ds(pl.multiple_of(s * 128, 128), 128)
        text_rows = pl.ds(pl.multiple_of(s * 256, 256), 256)
        keys = kvbuf[image_rows, :HD]
        values = kvbuf[image_rows, HD:]
        qs = query_ref[h, text_rows]
        hg = (factor * cot_ref[h, text_rows].astype(F32)).astype(BF16)
        e = jnp.exp(nt(keys, qs) * SCALE + bias_ref[s])
        total = jnp.sum(e, axis=0, keepdims=True)
        probs = e * (1.0 / jnp.where(total > 0.0, total, 1.0))
        probs_b = probs.astype(BF16)
        att_ref[h, text_rows] = (factor * tn(probs_b, values)).astype(BF16)
        dkv[image_rows, HD:] = nn(probs_b, hg).astype(BF16)
        pg = nt(values, hg)
        delta = jnp.sum(probs * pg, axis=0, keepdims=True)
        sg = (probs * (pg - delta) * SCALE).astype(BF16)
        dkv[image_rows, :HD] = nn(sg, qs).astype(BF16)

    def out_copy(h):
        return pltpu.make_async_copy(abuf.at[h], att_out.at[0, :, pl.ds(h * HD, HD)], lo.at[h])

    place, peers = (section, p, y, x, c), (sib, partner, at_y, at_x)
    reduce = reduction(acc, bufs, sems, place, peers)
    reduce2 = reduction(acc2, bufs2, sems2, place, peers)

    relay(2, 0, inner)
    relay(2, 1, inner)

    @pl.when(inner)
    def _():
        for t in range(NY):
            xcopy2(lax.rem(y + t, NY), 2, 1 - c).wait_recv()
        lend(1).wait_recv()
        lend(2).wait_recv()
        project(0, xbuf2)
        for s in range(SAMPLES):
            attend(0, s, lent)
        acc2[...] = nt(dkv[...], wbuf[0])
        for k in range(SAMPLES):
            reduce2["pair"](k)

    relay(2, 2, inner)
    relay_sides(1, HEADS - 1, p == 2, p == 1)

    @pl.when(inner)
    def _():
        for k in range(SAMPLES):
            reduce2["along_x"](k)
        project(0, xbuf)
        for s in range(SAMPLES):
            attend(0, s)
        out_copy(0).start()
        acc[...] += nt(dkv[...], wbuf[0])

    relay(2, HEADS - 1, inner)

    @pl.when(inner)
    def _():
        give_back().start()

    for h in range(1, HEADS - 1):
        ready(h)
        for s in range(SAMPLES):
            attend(h, s)
        out_copy(h).start()
        acc[...] += nt(dkv[...], wbuf[h])

        if h == HEADS - 2:

            @pl.when(inner)
            def _():
                for k in range(SAMPLES):
                    reduce2["along_y"](k)

    ready(HEADS - 1)
    for k in range(SAMPLES):
        s = sample_at(y, k)
        attend(HEADS - 1, s)
        rows = pl.ds(pl.multiple_of(s * 128, 128), 128)
        acc[rows] += nt(dkv[rows], wbuf[HEADS - 1])
        reduce["pair"](k)
        if k:
            reduce["along_x"](k - 1)
    reduce["along_x"](SAMPLES - 1)
    out_copy(HEADS - 1).start()

    @pl.when(inner)
    def _():
        mine2[...] = reduce2["owned"]().astype(BF16)
        give_sum().start()

    for k in range(SAMPLES):
        reduce["along_y"](k)

    @pl.when(end)
    def _():
        give_sum().wait_recv()

    reduce["planes"](more)

    @pl.when(end)
    def _():
        give_back().wait_recv()
        out_copy(0).start()

    reduce["spread"]()
    reduce["collect"](obuf)
    last = pltpu.make_async_copy(obuf, vis_out, lsem.at[1])
    last.start()

    for h in range(HEADS):
        for q in range(NZ):
            from_right = jnp.logical_and(send_left(h), p <= q)
            from_left = jnp.logical_and(send_right(h), p >= q)

            @pl.when(from_right)
            def _():
                zcopy(q, h, 0).wait_send()

            @pl.when(from_left)
            def _():
                zcopy(q, h, 1).wait_send()

    xcopy(y, 0, c).wait_send()
    xcopy(y, 1, c).wait_send()
    for t in range(1, 5):
        step_sent(t, xcopy)

    @pl.when(inner)
    def _():
        for to in range(3):
            xcopy2(y, to, c).wait_send()
        for t in range(1, 5):
            step_sent(t, xcopy2)
        give_back().wait_send()
        give_sum().wait_send()
        reduce2["shared_sent"]()

    @pl.when(end)
    def _():
        for i in range(3):
            lend(i).wait_send()

    reduce["sent"]()
    for h in range(HEADS):
        out_copy(h).wait()
    last.wait()


def shards(vision_tokens, key_weight, value_weight, queries, gate, visible, out_grad):
    dma = pltpu.SemaphoreType.DMA
    hbm = pl.BlockSpec(memory_space=pltpu.HBM)
    smem = pl.BlockSpec(memory_space=pltpu.SMEM)
    return pl.pallas_call(
        kernel,
        out_shape=(
            jax.ShapeDtypeStruct(queries.shape, BF16),
            jax.ShapeDtypeStruct(vision_tokens.shape, BF16),
        ),
        in_specs=[smem, smem, hbm, hbm, hbm, hbm, hbm],
        out_specs=(pl.BlockSpec(memory_space=pl.ANY),) * 2,
        scratch_shapes=[
            pltpu.VMEM((HEADS, DV, 2 * HD), BF16),
            pltpu.VMEM((VT, DV), BF16),
            pltpu.VMEM((HEADS, 1024, HD), BF16),
            pltpu.VMEM((HEADS, 1024, HD), BF16),
            pltpu.VMEM((HEADS, 1024, HD), BF16),
            pltpu.VMEM((SAMPLES, 128, 256), F32),
            pltpu.VMEM((VT, 2 * HD), BF16),
            pltpu.VMEM((VT, 2 * HD), BF16),
            pltpu.VMEM((VT, DV), F32),
            pltpu.VMEM((VT, DV), BF16),
            pltpu.VMEM((1, 1024, HD), BF16),
            pltpu.VMEM((1, 1024, HD), BF16),
            pltpu.VMEM((1, 1024, HD), BF16),
            pltpu.VMEM((SAMPLES, 128, 256), F32),
            pltpu.VMEM((VT, DV), F32),
            pltpu.VMEM((16, SHARE), BF16),
            pltpu.VMEM((16, SHARE), BF16),
            pltpu.VMEM((64, DV), BF16),
            reduction_bufs(),
            reduction_bufs(),
            dma((2,)),
            dma((HEADS, 2)),
            dma((HEADS,)),
            dma((HEADS,)),
            dma((HEADS,)),
            dma((2, NZ, HEADS)),
            dma((NZ, HEADS)),
            [dma((3, NY)), dma((NY,)), dma((NY,))],
            [dma((3, NY)), dma((NY,)), dma((NY,))],
            dma((5,)),
            dma((5,)),
            reduction_sems(),
            reduction_sems(),
        ],
        compiler_params=pltpu.CompilerParams(
            collective_id=0, has_side_effects=True, vmem_limit_bytes=60 * 2**20
        ),
        cost_estimate=pl.CostEstimate(flops=4 * 10**9, bytes_accessed=5 * 10**6, transcendentals=2**19),
    )(gate, visible, vision_tokens, key_weight, value_weight, queries, out_grad)


def solution(mesh):
    placed = (
        P("section", None),
        P("section", "tensor"),
        P("section", "tensor"),
        P("section", None, "tensor"),
        P(),
        P(),
        P("section", None, "tensor"),
    )
    return jax.shard_map(
        shards,
        mesh=mesh,
        in_specs=placed,
        out_specs=(P("section", None, "tensor"), P("section", None)),
        check_vma=False,
    )
```
